32 devices in a mesh: dp: 2 (over y), expert: 4 (over x, core), tensor: 4 (over z).
Axes of the slice: x: 2, y: 2, z: 4, core: 2. Of those that a mesh axis runs over, the one named last changes fastest.
Arguments:
- hidden: bfloat16 [1024, 2048], P(('dp', 'expert')), may hold values from -6 to 6
- out_grad: bfloat16 [1024, 7168], P(('dp', 'expert'), 'tensor'), may hold values from -6 to 6
- w_down: bfloat16 [4, 2048, 7168], P('expert', None, 'tensor'), may hold values from -0.125 to 0.125
- routes: int32 [1024, 1], P(('dp', 'expert')), may hold values from 0 to 3; in each aligned block of 128 rows (0 to 127, 128 to 255, ...) at most 64 rows name the same one
- placement: int32 [4], replicated, may hold values from 0 to 3, as said below
Outputs:
- output: bfloat16 [1024, 7168], P(('dp', 'expert'), 'tensor')
- d_hidden: bfloat16 [1024, 2048], P(('dp', 'expert'), 'tensor')
- d_weight: bfloat16 [4, 2048, 7168], P('expert', 'dp', 'tensor')
The draws below stay inside these ranges and needn't reach their ends.
Inputs may be any that keep to these rules, and one draw needn't show every extreme that they name: `routes`: among the 128 tokens of one index pair of dp and expert, no expert is named more than 64 times, a bound that some block reaches. `placement`: each expert is held at exactly one index.
All inputs are finite; a program needn't handle non-finite values.
Results may differ from the reference program's by a relative error of at most 0.009.
Values may be sent and summed in bfloat16 or wider, within the bound.
No kernel may reach another device: no remote copies, remote signals or barrier semaphores. Data moves between devices by JAX's collectives and lax.ppermute only.
A program may use at most 64 MiB of HBM per device.

```python
import math
import jax
import jax.numpy as jnp
import numpy as np
from jax import lax

D = 7168
FF = 2048
TOK_DEV = 128
EXPERTS = 4
CAP = 64
TOKENS = 1024
N_DP = 2
N_EXPERT = 4


def draw_placement(key, part):
    return jax.random.permutation(jax.random.fold_in(key, 7919), EXPERTS).astype(jnp.int32)


def block_scale(stream_key, dims, cuts, smallest, high):
    loudness, own = 1.0, jax.random.fold_in(stream_key, 6)
    for axis_at, parts in cuts:
        heights = jnp.exp(jax.random.uniform(jax.random.fold_in(own, axis_at), (parts,), jnp.float32, smallest / len(cuts), high / len(cuts)))
        loudness = loudness * jnp.repeat(heights, dims[axis_at] // parts).reshape([-1 if axis == axis_at else 1 for axis in range(len(dims))])
    return loudness


def assign_block(rng, own, number, rows, amount, top, most, lean):
    ranking = jax.random.permutation(rng, amount)
    heavy_load, ordinary = load_shares(amount, rows * top, most, lean, True), load_shares(amount, rows * top, most, lean, False)
    places = jnp.arange(amount)

    def named(lengths, turn):
        used = int((lengths > 0).sum())
        fixed = max(1, used // 4)
        moved = fixed + (places - fixed + turn * (used - fixed)) % max(1, amount - fixed)
        return jnp.zeros((amount,), jnp.int32).at[ranking[jnp.where(places < fixed, places, moved)]].set(jnp.asarray(lengths, jnp.int32))

    lengths = jnp.where(number % 4 == 0, named(heavy_load, number // 4), named(ordinary, number - number // 4 - 1))
    mixed = jax.random.permutation(jax.random.fold_in(own, 3), amount)
    giver, taker = mixed[0:amount // 2 * 2:2], mixed[1:amount // 2 * 2:2]
    margin = jnp.minimum(lengths[giver] - 1, most - lengths[taker]) // 2
    margin = jnp.where((giver == ranking[0]) | (taker == ranking[0]) | (lengths[taker] == 0), 0, jnp.maximum(margin, 0))
    moved = jax.random.randint(jax.random.fold_in(own, 4), (amount // 2,), 0, 1 << 20) % (margin + 1)
    lengths = lengths.at[giver].add(-moved).at[taker].add(moved)
    labels = jnp.searchsorted(jnp.cumsum(lengths), jnp.arange(rows * top), side="right").astype(jnp.int32)
    listing = labels.reshape(top, rows).T
    listing = listing[jax.random.permutation(jax.random.fold_in(own, 1), rows)]
    turn = jax.random.randint(jax.random.fold_in(own, 2), (rows, 1), 0, top)
    return jnp.take_along_axis(listing, (jnp.arange(top)[None, :] + turn) % top, axis=1)


def load_shares(number_of, total, most, lean, full):
    loads = [(1 << 20) // math.isqrt(rank ** lean) + 1 for rank in range(1, number_of + 1)]
    largest = most if full else min(most, max(-(-total // number_of), total * loads[0] // sum(loads)))
    least = 1 if total - largest >= number_of - 1 else 0
    given, rest = [largest] + [least] * (number_of - 1), total - largest - least * (number_of - 1)
    while rest > 0:
        free = [i for i in range(1, number_of) if given[i] < largest] or [i for i in range(1, number_of) if given[i] < most]
        whole, left = sum([loads[i] for i in free]), rest
        for i in free:
            extra = min(most - given[i], max(1, left * loads[i] // whole), rest)
            given[i] = given[i] + extra
            rest = rest - extra
    return np.array(given)


def centred(stream_key, extent, width, most, split=(), kind=jnp.bfloat16):
    entries = jax.random.normal(stream_key, extent, jnp.float32) * width
    if len(split) > 0:
        entries = block_scale(stream_key, extent, split, -0.22, 0.18) * entries
    return jnp.clip(entries, min=-most, max=most).astype(kind)


def setup_inputs(seed: int = 0) -> dict:
    seeds = jax.random.split(jax.random.key(seed), 6)
    hidden = centred(seeds[0], (TOKENS, FF), 1.0, 6.0, ((0, 8),))
    out_grad = centred(seeds[1], (TOKENS, D), 1.0, 6.0, ((0, 8), (1, 4)))
    w_down = centred(seeds[2], (EXPERTS, FF, D), FF ** -0.5, 0.125, ((0, 4), (2, 4)))
    routes_keys = jax.random.split(jax.random.fold_in(seeds[3], 1), TOKENS // TOK_DEV)
    routes_turns = jax.random.permutation(jax.random.fold_in(seeds[3], 3), TOKENS // TOK_DEV)
    routes = jax.vmap(lambda own, number: assign_block(jax.random.fold_in(seeds[3], 2), own, number, TOK_DEV, EXPERTS, 1, CAP, 2))(routes_keys, routes_turns).reshape((TOKENS, 1))
    placement = draw_placement(jax.random.fold_in(seeds[5], 71), 0)
    return dict(hidden=hidden, out_grad=out_grad, w_down=w_down, routes=routes, placement=placement)


def reference(hidden, out_grad, w_down, routes, placement):
    per = TOKENS // N_DP
    limit = N_EXPERT * CAP
    slot = jnp.take(placement, routes[:, 0]).astype(jnp.int32)
    slot_groups = slot.reshape(N_DP, per)
    hidden_pad = jnp.concatenate([hidden.reshape(N_DP, per, FF), jnp.zeros((N_DP, 1, FF), hidden.dtype)], axis=1)
    grad_pad = jnp.concatenate([out_grad.reshape(N_DP, per, D), jnp.zeros((N_DP, 1, D), out_grad.dtype)], axis=1)

    def expert(s):
        weight = w_down[s]
        total = jnp.zeros((FF, D), jnp.float32)
        outs, grads, places = [], [], []
        for group in range(N_DP):
            index = jnp.nonzero(slot_groups[group] == s, size=limit, fill_value=per)[0].astype(jnp.int32)
            rows_h = hidden_pad[group][index]
            rows_g = grad_pad[group][index]
            outs.append(jnp.dot(rows_h, weight, preferred_element_type=jnp.float32).astype(jnp.bfloat16))
            grads.append(jnp.dot(rows_g, weight.T, preferred_element_type=jnp.float32).astype(jnp.bfloat16))
            part = jnp.dot(rows_h.T, rows_g, preferred_element_type=jnp.float32).astype(jnp.bfloat16)
            total = total + part.astype(jnp.float32)
            places.append(jnp.where(index == per, TOKENS, index + group * per).astype(jnp.int32))
        return jnp.stack(outs), jnp.stack(grads), jnp.stack(places), total.astype(jnp.bfloat16)

    outs, grads, places, d_weight = lax.map(expert, jnp.arange(N_EXPERT, dtype=jnp.int32))
    flat = places.reshape(-1)
    output = jnp.zeros((TOKENS, D), jnp.bfloat16).at[flat].set(outs.reshape(-1, D), mode="drop")
    d_hidden = jnp.zeros((TOKENS, FF), jnp.bfloat16).at[flat].set(grads.reshape(-1, FF), mode="drop")
    return output, d_hidden, d_weight
```

```python
import jax
import jax.numpy as jnp
from jax import lax
from jax.sharding import PartitionSpec as P


def swap(value, axis, offset):
    size = lax.axis_size(axis)
    return lax.ppermute(value, axis, [(i, i ^ offset) for i in range(size)])


def route(routes, placement, experts, cap):
    chosen = routes == jnp.arange(placement.shape[0], dtype=jnp.int32)[None, :]
    target = jnp.sum(jnp.where(chosen, placement[None, :], 0), axis=1)
    landing = target[:, None] == jnp.arange(experts, dtype=jnp.int32)[None, :]
    counted = jnp.cumsum(landing.astype(jnp.int32), axis=0) - 1
    within = jnp.sum(jnp.where(landing, counted, 0), axis=1)
    return target, within


def few(hidden, out_grad, w_down, routes, placement):
    experts = lax.axis_size("expert")
    tensors = lax.axis_size("tensor")
    tok, width = hidden.shape
    cols = out_grad.shape[1]
    cap = 2 * tok // experts
    slots = experts * cap
    near = experts // 2 * cap
    target, within = route(routes, placement, experts, cap)
    me = lax.axis_index("expert")
    position = jnp.bitwise_xor(target, me) * cap + within
    picker = (jnp.arange(slots, dtype=jnp.int32)[:, None] == position[None, :]).astype(jnp.bfloat16)
    send_grad = jnp.dot(picker, out_grad, preferred_element_type=jnp.float32).astype(jnp.bfloat16)
    send_hidden = jnp.dot(picker, hidden, preferred_element_type=jnp.float32).astype(jnp.bfloat16)

    def exchange(value):
        blocks = [value[k * cap : (k + 1) * cap] for k in range(experts)]
        return [blocks[0]] + [swap(blocks[k], "expert", k) for k in range(1, experts)]

    grad = exchange(send_grad)
    hid = exchange(send_hidden)
    weight = w_down[0]
    half = experts // 2
    share = width // lax.axis_size("dp")
    column = width // tensors
    mine = lax.axis_index("dp") * share
    z = lax.axis_index("tensor")
    outs, backs, rows_h, rows_g = [], [], [], []
    for group in range(2):
        g = jnp.concatenate(grad[group * half : (group + 1) * half], axis=0)
        h = jnp.concatenate(hid[group * half : (group + 1) * half], axis=0)
        partial = lax.dot_general(g, weight, (((1,), (1,)), ((), ())), preferred_element_type=jnp.float32)
        partial = partial.astype(jnp.bfloat16)
        total = lax.dynamic_slice_in_dim(partial, z * column, column, 1).astype(jnp.float32)
        for k in range(1, tensors):
            piece = lax.dynamic_slice_in_dim(partial, jnp.bitwise_xor(z, k) * column, column, 1)
            total = total + swap(piece, "tensor", k).astype(jnp.float32)
        total = total.astype(jnp.bfloat16)
        out = jnp.dot(h, weight, preferred_element_type=jnp.float32).astype(jnp.bfloat16)
        for k in range(half):
            offset = group * half + k
            for value, into in ((out, outs), (total, backs)):
                block = value[k * cap : (k + 1) * cap]
                into.append(swap(block, "expert", offset) if offset else block)
        rows_h.append(lax.dynamic_slice_in_dim(h, mine, share, 1))
        rows_g.append(g)
        for k in range(1, lax.axis_size("dp")):
            other = jnp.bitwise_xor(lax.axis_index("dp"), k) * share
            rows_h.append(swap(lax.dynamic_slice_in_dim(h, other, share, 1), "dp", k))
            rows_g.append(swap(g, "dp", k))

    def place(blocks):
        return jnp.einsum(
            "rt,rd->td", picker, jnp.concatenate(blocks, axis=0), preferred_element_type=jnp.float32
        ).astype(jnp.bfloat16)

    d_weight = lax.dot_general(
        jnp.concatenate(rows_h, axis=0),
        jnp.concatenate(rows_g, axis=0),
        (((0,), (0,)), ((), ())),
        preferred_element_type=jnp.float32,
    ).astype(jnp.bfloat16)[None]
    return place(outs), place(backs), d_weight


def many(hidden, out_grad, w_down, routes, placement):
    experts = lax.axis_size("expert")
    tok = hidden.shape[0]
    width = hidden.shape[1]
    cols = out_grad.shape[1]
    cap = 2 * tok // experts
    slots = experts * cap
    target, within = route(routes, placement, experts, cap)
    position = target * cap + within
    picker = (jnp.arange(slots, dtype=jnp.int32)[:, None] == position[None, :]).astype(jnp.bfloat16)
    send_hidden = jnp.dot(picker, hidden, preferred_element_type=jnp.float32).astype(jnp.bfloat16)
    send_grad = jnp.dot(picker, out_grad, preferred_element_type=jnp.float32).astype(jnp.bfloat16)

    def exchange(value):
        return lax.all_to_all(
            value.reshape(experts, cap, -1), "expert", split_axis=0, concat_axis=0, tiled=True
        ).reshape(slots, -1)

    slot_hidden, slot_grad = exchange(send_hidden), exchange(send_grad)
    weight = w_down[0]
    out_rows = jnp.dot(slot_hidden, weight, preferred_element_type=jnp.float32).astype(jnp.bfloat16)
    partial_value = lax.dot_general(
        slot_grad, weight, (((1,), (1,)), ((), ())), preferred_element_type=jnp.float32
    )
    hidden_grad = lax.psum_scatter(partial_value, "tensor", scatter_dimension=1, tiled=True).astype(
        jnp.bfloat16
    )

    def place(rows):
        return jnp.einsum("rt,rd->td", picker, rows, preferred_element_type=jnp.float32).astype(jnp.bfloat16)

    output, d_hidden = place(exchange(out_rows)), place(exchange(hidden_grad))
    share = width // lax.axis_size("dp")
    mine = lax.axis_index("dp") * share
    part_h = lax.dynamic_slice_in_dim(
        lax.all_gather(slot_hidden, "dp", axis=0, tiled=True), mine, share, 1
    ).reshape(-1, slots, share)
    part_g = lax.all_gather(slot_grad, "dp", axis=0, tiled=True).reshape(-1, slots, cols)
    terms = jnp.einsum("krf,krd->kfd", part_h, part_g, preferred_element_type=jnp.float32)
    rounded = lax.optimization_barrier(terms.astype(jnp.bfloat16))
    summed = jnp.sum(rounded.astype(jnp.float32), axis=0)
    return output, d_hidden, summed.astype(jnp.bfloat16)[None]


def solution(mesh):
    in_specs = (
        P(("dp", "expert"), None),
        P(("dp", "expert"), "tensor"),
        P("expert", None, "tensor"),
        P(("dp", "expert"), None),
        P(),
    )
    out_specs = (
        P(("dp", "expert"), "tensor"),
        P(("dp", "expert"), "tensor"),
        P("expert", "dp", "tensor"),
    )
    small = all(mesh.shape[a] in (2, 4) for a in ("dp", "expert", "tensor"))
    shards = few if small else many
    return jax.shard_map(shards, mesh=mesh, in_specs=in_specs, out_specs=out_specs, check_vma=False)
```

```python
import functools

import jax
import jax.numpy as jnp
from jax import lax
from jax.experimental import pallas as pl
from jax.experimental.pallas import tpu as pltpu
from jax.sharding import PartitionSpec as P

VMEM = pl.BlockSpec(memory_space=pltpu.VMEM)
ANY = pl.BlockSpec(memory_space=pl.ANY)


def call(kernel, outs, ins, specs=None, scratch=(), after=(), cost=0, out_specs=None):
    def late(*refs):
        kernel(*refs[: len(ins)], *refs[len(ins) + len(after) :])

    return pl.pallas_call(
        late,
        out_shape=tuple(jax.ShapeDtypeStruct(s, d) for s, d in outs),
        in_specs=[*(specs or [VMEM] * len(ins)), *[ANY] * len(after)],
        out_specs=tuple(out_specs or [VMEM] * len(outs)),
        scratch_shapes=list(scratch),
        cost_estimate=pl.CostEstimate(flops=1000, bytes_accessed=1000 + cost, transcendentals=0),
        compiler_params=pltpu.CompilerParams(vmem_limit_bytes=24 << 20),
    )(*ins, *after)


def far(value):
    return pltpu.with_memory_space_constraint(value, pltpu.HBM)


def swap(value, axis, offset):
    size = lax.axis_size(axis)
    return lax.ppermute(value, axis, [(i, i ^ offset) for i in range(size)])


def route(routes, placement, experts, cap):
    chosen = routes == jnp.arange(placement.shape[0], dtype=jnp.int32)[None, :]
    target = jnp.sum(jnp.where(chosen, placement[None, :], 0), axis=1)
    landing = target[:, None] == jnp.arange(experts, dtype=jnp.int32)[None, :]
    counted = jnp.cumsum(landing.astype(jnp.int32), axis=0) - 1
    within = jnp.sum(jnp.where(landing, counted, 0), axis=1)
    return target, within


def slot_of(routes, placement, owner, experts, cap):
    tok = routes.shape[1]
    target = jnp.zeros((1, tok), jnp.int32)
    for j in range(experts):
        target = jnp.where(routes == j, placement[j], target)
    key = jnp.bitwise_xor(target, owner)
    landing = jnp.where(key == lax.broadcasted_iota(jnp.int32, (max(8, experts), tok), 0), 1.0, 0.0)
    earlier = lax.broadcasted_iota(jnp.int32, (tok, tok), 0) <= lax.broadcasted_iota(jnp.int32, (tok, tok), 1)
    counted = jnp.dot(
        landing.astype(jnp.bfloat16),
        jnp.where(earlier, 1.0, 0.0).astype(jnp.bfloat16),
        preferred_element_type=jnp.float32,
    )
    within = jnp.sum(landing * counted, axis=0, keepdims=True).astype(jnp.int32) - 1
    position = key * cap + within
    slots = lax.broadcasted_iota(jnp.int32, (experts * cap, tok), 0)
    return jnp.where(position == slots, 1.0, 0.0).astype(jnp.bfloat16)


def weight_copies(tensors, first, weight, held, sem):
    rows = held.shape[1]
    copies = []
    for i in range(tensors // 2):
        block = jnp.bitwise_xor(lax.axis_index("tensor"), first + 2 * i)
        start = pl.multiple_of(block * rows, rows)
        copies.append(pltpu.make_async_copy(weight.at[0, pl.ds(start, rows)], held.at[i], sem.at[i]))
    return copies


def chosen(slot, value):
    return jnp.dot(slot, value, preferred_element_type=jnp.float32).astype(jnp.bfloat16)


def pick(tensors, cap, *refs):
    routes, placement, grad, hid, weight, next_routes, next_grad, next_hid = refs[:8]
    slot_out, next_slot_out, hid_out, odd, near_g, near_h, far_g, near_pack = refs[8:16]
    routes_held, placement_held, grad_held, sem, weight_sem = refs[16:]
    copies = [
        pltpu.make_async_copy(*pair, sem.at[i])
        for i, pair in enumerate(
            ((routes, routes_held), (placement, placement_held), (grad, grad_held), (hid, hid_out))
        )
    ]
    halves = weight_copies(tensors, 1, weight, odd, weight_sem)
    for copy in copies + halves:
        copy.start()
    copies[0].wait()
    copies[1].wait()
    me = lax.axis_index("expert")
    experts = placement.shape[0]
    slot = slot_of(routes_held[...], placement_held, me, experts, cap)
    next_slot = slot_of(next_routes[...], placement_held, jnp.bitwise_xor(me, 1), experts, cap)
    slot_out[...] = slot
    next_slot_out[...] = next_slot
    copies[2].wait()
    far_g[:cap] = chosen(slot[2 * cap : 3 * cap], grad_held[...])
    far_g[cap:] = chosen(next_slot[3 * cap :], next_grad[...])
    near_g[:cap] = chosen(slot[:cap], grad_held[...])
    near_g[cap:] = chosen(next_slot[cap : 2 * cap], next_grad[...])
    copies[3].wait()
    near_h[:cap] = chosen(slot[:cap], hid_out[...])
    near_h[cap:] = chosen(next_slot[cap : 2 * cap], next_hid[...])
    cols, share = near_g.shape[1], near_h.shape[1] // 2
    near_pack[:, :cols] = near_g[...]
    near_pack[:, cols:] = near_h[:, other_share(share)]
    for copy in halves:
        copy.wait()


def pick_far(cap, slot, hid, next_slot, next_hid, out):
    out[:cap] = chosen(slot[2 * cap : 3 * cap], hid[...])
    out[cap:] = chosen(next_slot[3 * cap :], next_hid[...])


def own_share(share):
    return pl.ds(pl.multiple_of(lax.axis_index("dp") * share, share), share)


def other_share(share):
    return pl.ds(pl.multiple_of((1 - lax.axis_index("dp")) * share, share), share)


def cut_other(hid, out):
    out[...] = hid[:, other_share(out.shape[1])]


def hidden_grad(weight, grads, out):
    blocks, rows, _ = weight.shape
    for i in range(blocks):
        part = lax.dot_general(
            grads[...], weight[i], (((1,), (1,)), ((), ())), preferred_element_type=jnp.float32
        )
        out[:, i * rows : (i + 1) * rows] = part.astype(out.dtype)


def output_rows(first, weight, hids, total=None):
    blocks, rows, _ = weight.shape
    for i in range(blocks):
        block = jnp.bitwise_xor(lax.axis_index("tensor"), first + 2 * i)
        start = pl.multiple_of(block * rows, rows)
        term = jnp.dot(hids[:, pl.ds(start, rows)], weight[i], preferred_element_type=jnp.float32)
        total = term if total is None else total + term
    return total


def near_rows(tensors, weight, odd, grads, hids, even, keep, send, out, sem):
    copies = weight_copies(tensors, 0, weight, even, sem)
    for copy in copies:
        copy.start()
    hidden_grad(odd, grads, send)
    total = output_rows(1, odd, hids)
    for copy in copies:
        copy.wait()
    hidden_grad(even, grads, keep)
    out[...] = output_rows(0, even, hids, total).astype(out.dtype)


def cut_rows(total, outs):
    rows = outs[0].shape[0]
    for i, out in enumerate(outs):
        out[...] = total[i * rows : (i + 1) * rows].astype(out.dtype)


def far_grads(odd, even, grads, keep, send):
    hidden_grad(odd, grads, send)
    hidden_grad(even, grads, keep)


def far_outs(odd, even, hids, *outs):
    cut_rows(output_rows(0, even, hids, output_rows(1, odd, hids)), outs)


def fold(keep, got, *outs):
    total = keep[...] + got[...].astype(jnp.float32)
    if outs[0].dtype == jnp.float32:
        cut = outs[0].shape[1]
        outs[0][...] = total[:, :cut]
        outs[1][...] = total[:, cut:].astype(outs[1].dtype)
    else:
        cut_rows(total, outs)


def place(cap, slot, *refs):
    *rows, out, token = refs
    rows = [ref[...] if ref.shape[0] == cap else ref[i % 2 * cap : (i % 2 + 1) * cap] for i, ref in enumerate(rows)]
    out[...] = lax.dot_general(
        slot[...], jnp.concatenate(rows, axis=0), (((0,), (0,)), ((), ())), preferred_element_type=jnp.float32
    ).astype(out.dtype)
    token[...] = jnp.zeros_like(token)


def joined(grads, hids, other_g, other_h):
    g = jnp.concatenate([grads[...], other_g[...]], axis=0)
    h = jnp.concatenate([hids[:, own_share(other_h.shape[1])], other_h[...]], axis=0)
    return g, h


def outer_near(grads, hids, both, out):
    cols = grads.shape[1]
    g, h = joined(grads, hids, both.at[:, :cols], both.at[:, cols:])
    out[...] = lax.dot_general(h, g, (((0,), (0,)), ((), ())), preferred_element_type=jnp.float32)


def outer_far(near, grads, hids, other_g, other_h, out, token, held, sem):
    g, h = joined(grads, hids, other_g, other_h)
    pieces, rows, _ = held.shape
    copies = []
    for i in range(pieces):
        part = slice(i * rows, (i + 1) * rows)
        term = lax.dot_general(h[:, part], g, (((0,), (0,)), ((), ())), preferred_element_type=jnp.float32)
        held[i] = (near[part] + term).astype(held.dtype)
        copies.append(pltpu.make_async_copy(held.at[i], out.at[0, pl.ds(i * rows, rows)], sem.at[i]))
        copies[i].start()
    token[...] = jnp.zeros_like(token)
    for copy in copies:
        copy.wait()


def few(hidden, out_grad, w_down, routes, placement):
    experts = lax.axis_size("expert")
    tensors = lax.axis_size("tensor")
    tok, width = hidden.shape
    cols = out_grad.shape[1]
    cap = 2 * tok // experts
    slots = experts * cap
    share = width // 2
    column = width // tensors
    bf, f32 = jnp.bfloat16, jnp.float32
    rows = 2 * cap
    kept, cut, token = (rows, width // 2), (rows, column), ((8, 128), f32)
    part = ((tensors // 2, column, cols), bf)
    pair = ((cap, column), bf)

    routes = routes.reshape(1, tok)
    next_routes, next_grad, next_hid = (swap(x, "expert", 1) for x in (routes, out_grad, hidden))
    slot, next_slot, held, odd, near_g, near_h, far_g, near_pack = call(
        functools.partial(pick, tensors, cap),
        [
            ((slots, tok), bf),
            ((slots, tok), bf),
            ((tok, width), bf),
            part,
            ((rows, cols), bf),
            ((rows, width), bf),
            ((rows, cols), bf),
            ((rows, cols + share), bf),
        ],
        (*(far(x) for x in (routes, placement, out_grad, hidden, w_down)), next_routes, next_grad, next_hid),
        [*[ANY] * 5, *[VMEM] * 3],
        [
            pltpu.VMEM((1, tok), jnp.int32),
            pltpu.SMEM((experts,), jnp.int32),
            pltpu.VMEM((tok, cols), bf),
            pltpu.SemaphoreType.DMA((4,)),
            pltpu.SemaphoreType.DMA((tensors // 2,)),
        ],
    )
    far_g = swap(far_g, "expert", 2)
    other_near = swap(near_pack, "dp", 1)
    even, near_keep, near_send, near_out = call(
        functools.partial(near_rows, tensors),
        [part, (kept, f32), (kept, bf), ((rows, cols), bf)],
        (far(w_down), odd, near_g, near_h),
        [ANY, *[VMEM] * 3],
        [pltpu.SemaphoreType.DMA((tensors // 2,))],
    )
    near_got = swap(near_send, "tensor", 1)
    (picked,) = call(
        functools.partial(pick_far, cap), [((rows, width), bf)], (slot, held, next_slot, next_hid), after=(near_send,)
    )
    far_h = swap(picked, "expert", 2)
    far_keep, far_send = call(
        far_grads, [(kept, f32), (kept, bf)], (odd, even, far_g), after=(picked,)
    )
    far_got = swap(far_send, "tensor", 1)
    other_g = swap(far_g, "dp", 1)
    last = far_send
    if tensors > 2:
        near_keep, near_send = call(fold, [(cut, f32), (cut, bf)], (near_keep, near_got), after=(last,))
        near_got = swap(near_send, "tensor", 2)
        last = near_send
    (near_total,) = call(outer_near, [((share, cols), f32)], (near_g, near_h, other_near), after=(last,))
    last = near_total
    if tensors > 2:
        far_keep, far_send = call(fold, [(cut, f32), (cut, bf)], (far_keep, far_got), after=(last,))
        far_got = swap(far_send, "tensor", 2)
        last = far_send
    next_out = swap(near_out, "expert", 1)
    far_out = call(far_outs, [((cap, cols), bf)] * 2, (odd, even, far_h), after=(last, next_out))
    (cut_h,) = call(cut_other, [((rows, share), bf)], (far_h,), after=(far_out[0],))
    other_h = swap(cut_h, "dp", 1)
    (near_back,) = call(fold, [(cut, bf)], (near_keep, near_got), after=(cut_h,))
    next_back = swap(near_back, "expert", 1)
    far_back = call(fold, [pair, pair], (far_keep, far_got), after=(next_back, other_g))
    output, last = call(
        functools.partial(place, cap),
        [((tok, cols), bf), token],
        (slot, near_out, next_out, swap(far_out[0], "expert", 2), swap(far_out[1], "expert", 3)),
        after=(far_back[0],),
    )
    pieces = 4
    d_weight, last = call(
        outer_far,
        [((1, share, cols), bf), token],
        (near_total, far_g, far_h, other_g, other_h),
        None,
        [pltpu.VMEM((pieces, share // pieces, cols), bf), pltpu.SemaphoreType.DMA((pieces,))],
        after=(last,),
        out_specs=[ANY, VMEM],
    )
    d_hidden, _ = call(
        functools.partial(place, cap),
        [((tok, column), bf), token],
        (
            slot,
            near_back,
            next_back,
            swap(far_back[0], "expert", 2),
            swap(far_back[1], "expert", 3),
        ),
        after=(last,),
    )
    return output, d_hidden, d_weight


def many(hidden, out_grad, w_down, routes, placement):
    experts = lax.axis_size("expert")
    tok = hidden.shape[0]
    width = hidden.shape[1]
    cols = out_grad.shape[1]
    cap = 2 * tok // experts
    slots = experts * cap
    target, within = route(routes, placement, experts, cap)
    position = target * cap + within
    picker = (jnp.arange(slots, dtype=jnp.int32)[:, None] == position[None, :]).astype(jnp.bfloat16)
    send_hidden = jnp.dot(picker, hidden, preferred_element_type=jnp.float32).astype(jnp.bfloat16)
    send_grad = jnp.dot(picker, out_grad, preferred_element_type=jnp.float32).astype(jnp.bfloat16)

    def exchange(value):
        return lax.all_to_all(
            value.reshape(experts, cap, -1), "expert", split_axis=0, concat_axis=0, tiled=True
        ).reshape(slots, -1)

    slot_hidden, slot_grad = exchange(send_hidden), exchange(send_grad)
    weight = w_down[0]
    out_rows = jnp.dot(slot_hidden, weight, preferred_element_type=jnp.float32).astype(jnp.bfloat16)
    partial_value = lax.dot_general(
        slot_grad, weight, (((1,), (1,)), ((), ())), preferred_element_type=jnp.float32
    )
    hidden_grad = lax.psum_scatter(partial_value, "tensor", scatter_dimension=1, tiled=True).astype(
        jnp.bfloat16
    )

    def place(rows):
        return jnp.einsum("rt,rd->td", picker, rows, preferred_element_type=jnp.float32).astype(jnp.bfloat16)

    output, d_hidden = place(exchange(out_rows)), place(exchange(hidden_grad))
    share = width // lax.axis_size("dp")
    mine = lax.axis_index("dp") * share
    part_h = lax.dynamic_slice_in_dim(
        lax.all_gather(slot_hidden, "dp", axis=0, tiled=True), mine, share, 1
    ).reshape(-1, slots, share)
    part_g = lax.all_gather(slot_grad, "dp", axis=0, tiled=True).reshape(-1, slots, cols)
    terms = jnp.einsum("krf,krd->kfd", part_h, part_g, preferred_element_type=jnp.float32)
    rounded = lax.optimization_barrier(terms.astype(jnp.bfloat16))
    summed = jnp.sum(rounded.astype(jnp.float32), axis=0)
    return output, d_hidden, summed.astype(jnp.bfloat16)[None]


def solution(mesh):
    in_specs = (
        P(("dp", "expert"), None),
        P(("dp", "expert"), "tensor"),
        P("expert", None, "tensor"),
        P(("dp", "expert"), None),
        P(),
    )
    out_specs = (
        P(("dp", "expert"), "tensor"),
        P(("dp", "expert"), "tensor"),
        P("expert", "dp", "tensor"),
    )
    small = mesh.shape["dp"] == 2 and mesh.shape["expert"] == 4 and mesh.shape["tensor"] in (2, 4)
    shards = few if small else many
    return jax.shard_map(shards, mesh=mesh, in_specs=in_specs, out_specs=out_specs, check_vma=False)
```

```python
import functools

import jax
import jax.numpy as jnp
from jax import lax
from jax.experimental import pallas as pl
from jax.experimental.pallas import tpu as pltpu
from jax.sharding import PartitionSpec as P

VMEM = pl.BlockSpec(memory_space=pltpu.VMEM)
ANY = pl.BlockSpec(memory_space=pl.ANY)


def call(kernel, outs, ins, specs=None, scratch=(), after=(), out_specs=None):
    name = getattr(kernel, "func", kernel).__name__

    def late(*refs):
        kernel(*refs[: len(ins)], *refs[len(ins) + len(after) :])

    return pl.pallas_call(
        late,
        out_shape=tuple(jax.ShapeDtypeStruct(s, d) for s, d in outs),
        in_specs=[*(specs or [VMEM] * len(ins)), *[ANY] * len(after)],
        out_specs=tuple(out_specs or [VMEM] * len(outs)),
        scratch_shapes=list(scratch),
        name=name,
        cost_estimate=pl.CostEstimate(flops=1000, bytes_accessed=1000, transcendentals=0),
        compiler_params=pltpu.CompilerParams(vmem_limit_bytes=24 << 20),
    )(*ins, *after)


def far(value):
    return pltpu.with_memory_space_constraint(value, pltpu.HBM)


def swap(value, axis, offset):
    size = lax.axis_size(axis)
    return lax.ppermute(value, axis, [(i, i ^ offset) for i in range(size)])


def route(routes, placement, experts, cap):
    chosen = routes == jnp.arange(placement.shape[0], dtype=jnp.int32)[None, :]
    target = jnp.sum(jnp.where(chosen, placement[None, :], 0), axis=1)
    landing = target[:, None] == jnp.arange(experts, dtype=jnp.int32)[None, :]
    counted = jnp.cumsum(landing.astype(jnp.int32), axis=0) - 1
    within = jnp.sum(jnp.where(landing, counted, 0), axis=1)
    return target, within


def slot_of(routes, placement, owner, experts, cap):
    tok = routes.shape[1]
    target = jnp.zeros((1, tok), jnp.int32)
    for j in range(experts):
        target = jnp.where(routes == j, placement[j : j + 1, :tok], target)
    key = jnp.bitwise_xor(target, owner)
    landing = jnp.where(key == lax.broadcasted_iota(jnp.int32, (max(8, experts), tok), 0), 1.0, 0.0)
    earlier = lax.broadcasted_iota(jnp.int32, (tok, tok), 0) <= lax.broadcasted_iota(jnp.int32, (tok, tok), 1)
    counted = jnp.dot(
        landing.astype(jnp.bfloat16),
        jnp.where(earlier, 1.0, 0.0).astype(jnp.bfloat16),
        preferred_element_type=jnp.float32,
    )
    within = jnp.sum(landing * counted, axis=0, keepdims=True).astype(jnp.int32) - 1
    position = key * cap + within
    slots = lax.broadcasted_iota(jnp.int32, (experts * cap, tok), 0)
    return jnp.where(position == slots, 1.0, 0.0).astype(jnp.bfloat16)


def chosen(slot, value):
    return jnp.dot(slot, value, preferred_element_type=jnp.float32).astype(jnp.bfloat16)


def pick_own(cap, routes, placement, grad, hid, slot_out, hid_out, near_g, near_h, far_g, table, *refs):
    routes_held, placement_held, grad_held, sem = refs
    copies = [
        pltpu.make_async_copy(*pair, sem.at[i])
        for i, pair in enumerate(
            ((routes, routes_held), (placement, placement_held), (grad, grad_held), (hid, hid_out))
        )
    ]
    for copy in copies:
        copy.start()
    copies[0].wait()
    copies[1].wait()
    experts = placement.shape[0]
    for j in range(experts):
        table[j : j + 1] = jnp.full((1, table.shape[1]), placement_held[j], jnp.int32)
    slot = slot_of(routes_held[...], table, lax.axis_index("expert"), experts, cap)
    slot_out[...] = slot
    copies[2].wait()
    far_g[...] = chosen(slot[2 * cap : 3 * cap], grad_held[...])
    near_g[...] = chosen(slot[:cap], grad_held[...])
    copies[3].wait()
    near_h[...] = chosen(slot[:cap], hid_out[...])


def pick_next(cap, *refs):
    table, routes, grad, hid, own_near_g, own_near_h, own_far_g = refs[:7]
    slot_out, near_g, near_h, far_g, near_pack = refs[7:]
    experts = slot_out.shape[0] // cap
    slot = slot_of(routes[...], table, jnp.bitwise_xor(lax.axis_index("expert"), 1), experts, cap)
    slot_out[...] = slot
    far_g[:cap] = own_far_g[...]
    far_g[cap:] = chosen(slot[3 * cap :], grad[...])
    near_g[:cap] = own_near_g[...]
    near_g[cap:] = chosen(slot[cap : 2 * cap], grad[...])
    near_h[:cap] = own_near_h[...]
    near_h[cap:] = chosen(slot[cap : 2 * cap], hid[...])
    cols, share = near_g.shape[1], near_h.shape[1] // 2
    near_pack[:, :cols] = near_g[...]
    near_pack[:, cols:] = near_h[:, other_share(share)]


def pick_far(cap, slot, hid, next_slot, next_hid, own, following):
    own[...] = chosen(slot[2 * cap : 3 * cap], hid[...])
    following[...] = chosen(next_slot[3 * cap :], next_hid[...])


def own_share(share):
    return pl.ds(pl.multiple_of(lax.axis_index("dp") * share, share), share)


def other_share(share):
    return pl.ds(pl.multiple_of((1 - lax.axis_index("dp")) * share, share), share)


def cut_other(first, second, out):
    rows = first.shape[0]
    out[:rows] = first[:, other_share(out.shape[1])]
    out[rows:] = second[:, other_share(out.shape[1])]


def hidden_grad(weight, i, grads, out):
    rows = weight.shape[1]
    part = lax.dot_general(grads[...], weight[i], (((1,), (1,)), ((), ())), preferred_element_type=jnp.float32)
    out[:, i * rows : (i + 1) * rows] = part.astype(out.dtype)


def output_rows(first, weight, hids, total):
    blocks, rows, _ = weight.shape
    for i in range(blocks):
        block = jnp.bitwise_xor(lax.axis_index("tensor"), first + 2 * i)
        start = pl.multiple_of(block * rows, rows)
        h = jnp.concatenate([ref[:, pl.ds(start, rows)] for ref in hids], axis=0)
        term = jnp.dot(h, weight[i], preferred_element_type=jnp.float32)
        total = term if total is None else total + term
    return total


def weight_copies(first, weight, held, sem):
    rows = held.shape[1]
    copies = []
    for i in range(held.shape[0]):
        block = jnp.bitwise_xor(lax.axis_index("tensor"), first + 2 * i)
        start = pl.multiple_of(block * rows, rows)
        copies.append(pltpu.make_async_copy(weight.at[0, pl.ds(start, rows)], held.at[i], sem.at[i]))
        copies[i].start()
    return copies


def near_odd(weight, grads, odd, send, sem):
    for i, copy in enumerate(weight_copies(1, weight, odd, sem)):
        copy.wait()
        hidden_grad(odd, i, grads, send)


def near_even(weight, odd, grads, hids, even, keep, own, following, sem):
    copies = weight_copies(0, weight, even, sem)
    total = output_rows(1, odd, [hids], None)
    for i, copy in enumerate(copies):
        copy.wait()
        hidden_grad(even, i, grads, keep)
    cut_rows(output_rows(0, even, [hids], total), (own, following))


def cut_rows(total, outs):
    rows = outs[0].shape[0]
    for i, out in enumerate(outs):
        out[...] = total[i * rows : (i + 1) * rows].astype(out.dtype)


def far_grads(weight, grads, out):
    for i in range(weight.shape[0]):
        hidden_grad(weight, i, grads, out)


def far_outs(odd, even, first, second, *outs):
    hids = first, second
    cut_rows(output_rows(0, even, hids, output_rows(1, odd, hids, None)), outs)


def fold(keep, got, *outs):
    total = keep[...] + got[...].astype(jnp.float32)
    if outs[0].dtype == jnp.float32:
        cut = outs[0].shape[1]
        outs[0][...] = total[:, :cut]
        outs[1][...] = total[:, cut:].astype(outs[1].dtype)
    else:
        cut_rows(total, outs)


def place(cap, slot, *refs):
    *rows, out, token = refs
    rows = [ref[...] if ref.shape[0] == cap else ref[i % 2 * cap : (i % 2 + 1) * cap] for i, ref in enumerate(rows)]
    out[...] = lax.dot_general(
        slot[...], jnp.concatenate(rows, axis=0), (((0,), (0,)), ((), ())), preferred_element_type=jnp.float32
    ).astype(out.dtype)
    token[...] = jnp.zeros_like(token)


def joined(grads, hids, other_g, other_h):
    g = jnp.concatenate([grads[...], other_g[...]], axis=0)
    part = own_share(other_h.shape[1])
    h = jnp.concatenate([*[ref[:, part] for ref in hids], other_h[...]], axis=0)
    return g, h


def outer_near(grads, hids, both, out):
    cols = grads.shape[1]
    g, h = joined(grads, [hids], both.at[:, :cols], both.at[:, cols:])
    out[...] = lax.dot_general(h, g, (((0,), (0,)), ((), ())), preferred_element_type=jnp.float32)


def outer_far(near, grads, first, second, other_g, other_h, out, token, held, sem):
    g, h = joined(grads, [first, second], other_g, other_h)
    pieces, rows, _ = held.shape
    copies = []
    for i in range(pieces):
        part = slice(i * rows, (i + 1) * rows)
        term = lax.dot_general(h[:, part], g, (((0,), (0,)), ((), ())), preferred_element_type=jnp.float32)
        held[i] = (near[part] + term).astype(held.dtype)
        copies.append(pltpu.make_async_copy(held.at[i], out.at[0, pl.ds(i * rows, rows)], sem.at[i]))
        copies[i].start()
    token[...] = jnp.zeros_like(token)
    for copy in copies:
        copy.wait()


def few(hidden, out_grad, w_down, routes, placement):
    experts = lax.axis_size("expert")
    tensors = lax.axis_size("tensor")
    tok, width = hidden.shape
    cols = out_grad.shape[1]
    cap = 2 * tok // experts
    slots = experts * cap
    share = width // 2
    column = width // tensors
    bf, f32 = jnp.bfloat16, jnp.float32
    rows = 2 * cap
    kept, cut, token = (rows, width // 2), (rows, column), ((8, 128), f32)
    pair = ((cap, column), bf)

    routes = routes.reshape(1, tok)
    next_routes, next_grad, next_hid = (swap(x, "expert", 1) for x in (routes, out_grad, hidden))
    slot, held, near_g, near_h, far_g, table = call(
        functools.partial(pick_own, cap),
        [
            ((slots, tok), bf),
            ((tok, width), bf),
            ((cap, cols), bf),
            ((cap, width), bf),
            ((cap, cols), bf),
            ((8, 128), jnp.int32),
        ],
        tuple(far(x) for x in (routes, placement, out_grad, hidden)),
        [ANY] * 4,
        [
            pltpu.VMEM((1, tok), jnp.int32),
            pltpu.SMEM((experts,), jnp.int32),
            pltpu.VMEM((tok, cols), bf),
            pltpu.SemaphoreType.DMA((4,)),
        ],
    )
    next_slot, near_g, near_h, far_g, near_pack = call(
        functools.partial(pick_next, cap),
        [
            ((slots, tok), bf),
            ((rows, cols), bf),
            ((rows, width), bf),
            ((rows, cols), bf),
            ((rows, cols + share), bf),
        ],
        (table, next_routes, next_grad, next_hid, near_g, near_h, far_g),
    )
    far_g = swap(far_g, "expert", 2)
    other_near = swap(near_pack, "dp", 1)
    part = ((tensors // 2, column, cols), bf)
    sems = [pltpu.SemaphoreType.DMA((tensors // 2,))]
    odd, near_send = call(
        near_odd, [part, (kept, bf)], (far(w_down), near_g), [ANY, VMEM], sems
    )
    near_got = swap(near_send, "tensor", 1)
    even, near_keep, near_out, next_out = call(
        near_even,
        [part, (kept, f32), ((cap, cols), bf), ((cap, cols), bf)],
        (far(w_down), odd, near_g, near_h),
        [ANY, *[VMEM] * 3],
        sems,
    )
    next_out = swap(next_out, "expert", 1)
    picked = call(
        functools.partial(pick_far, cap),
        [((cap, width), bf)] * 2,
        (slot, held, next_slot, next_hid),
        after=(near_keep,),
    )
    far_h = [swap(x, "expert", 2) for x in picked]
    (far_send,) = call(far_grads, [(kept, bf)], (odd, far_g), after=(picked[0],))
    far_got = swap(far_send, "tensor", 1)
    (far_keep,) = call(far_grads, [(kept, f32)], (even, far_g), after=(far_send,))
    other_g = swap(far_g, "dp", 1)
    last = far_keep
    if tensors > 2:
        near_keep, near_send = call(fold, [(cut, f32), (cut, bf)], (near_keep, near_got), after=(last,))
        near_got = swap(near_send, "tensor", 2)
        last = near_send
    far_out = call(far_outs, [((cap, cols), bf)] * 2, (odd, even, *far_h), after=(last, next_out))
    last = far_out[0]
    if tensors > 2:
        far_keep, far_send = call(fold, [(cut, f32), (cut, bf)], (far_keep, far_got), after=(last,))
        far_got = swap(far_send, "tensor", 2)
        last = far_send
    (near_total,) = call(outer_near, [((share, cols), f32)], (near_g, near_h, other_near), after=(last,))
    (cut_h,) = call(cut_other, [((rows, share), bf)], far_h, after=(near_total,))
    other_h = swap(cut_h, "dp", 1)
    (near_back,) = call(fold, [(cut, bf)], (near_keep, near_got), after=(cut_h,))
    next_back = swap(near_back, "expert", 1)
    far_back = call(fold, [pair, pair], (far_keep, far_got), after=(near_back, other_g))
    output, last = call(
        functools.partial(place, cap),
        [((tok, cols), bf), token],
        (slot, near_out, next_out, swap(far_out[0], "expert", 2), swap(far_out[1], "expert", 3)),
        after=(far_back[0],),
    )
    pieces = 4
    d_weight, last = call(
        outer_far,
        [((1, share, cols), bf), token],
        (near_total, far_g, *far_h, other_g, other_h),
        None,
        [pltpu.VMEM((pieces, share // pieces, cols), bf), pltpu.SemaphoreType.DMA((pieces,))],
        after=(last,),
        out_specs=[ANY, VMEM],
    )
    d_hidden, _ = call(
        functools.partial(place, cap),
        [((tok, column), bf), token],
        (
            slot,
            near_back,
            next_back,
            swap(far_back[0], "expert", 2),
            swap(far_back[1], "expert", 3),
        ),
        after=(last,),
    )
    return output, d_hidden, d_weight


def many(hidden, out_grad, w_down, routes, placement):
    experts = lax.axis_size("expert")
    tok = hidden.shape[0]
    width = hidden.shape[1]
    cols = out_grad.shape[1]
    cap = 2 * tok // experts
    slots = experts * cap
    target, within = route(routes, placement, experts, cap)
    position = target * cap + within
    picker = (jnp.arange(slots, dtype=jnp.int32)[:, None] == position[None, :]).astype(jnp.bfloat16)
    send_hidden = jnp.dot(picker, hidden, preferred_element_type=jnp.float32).astype(jnp.bfloat16)
    send_grad = jnp.dot(picker, out_grad, preferred_element_type=jnp.float32).astype(jnp.bfloat16)

    def exchange(value):
        return lax.all_to_all(
            value.reshape(experts, cap, -1), "expert", split_axis=0, concat_axis=0, tiled=True
        ).reshape(slots, -1)

    slot_hidden, slot_grad = exchange(send_hidden), exchange(send_grad)
    weight = w_down[0]
    out_rows = jnp.dot(slot_hidden, weight, preferred_element_type=jnp.float32).astype(jnp.bfloat16)
    partial_value = lax.dot_general(
        slot_grad, weight, (((1,), (1,)), ((), ())), preferred_element_type=jnp.float32
    )
    hidden_grad = lax.psum_scatter(partial_value, "tensor", scatter_dimension=1, tiled=True).astype(
        jnp.bfloat16
    )

    def place(rows):
        return jnp.einsum("rt,rd->td", picker, rows, preferred_element_type=jnp.float32).astype(jnp.bfloat16)

    output, d_hidden = place(exchange(out_rows)), place(exchange(hidden_grad))
    share = width // lax.axis_size("dp")
    mine = lax.axis_index("dp") * share
    part_h = lax.dynamic_slice_in_dim(
        lax.all_gather(slot_hidden, "dp", axis=0, tiled=True), mine, share, 1
    ).reshape(-1, slots, share)
    part_g = lax.all_gather(slot_grad, "dp", axis=0, tiled=True).reshape(-1, slots, cols)
    terms = jnp.einsum("krf,krd->kfd", part_h, part_g, preferred_element_type=jnp.float32)
    rounded = lax.optimization_barrier(terms.astype(jnp.bfloat16))
    summed = jnp.sum(rounded.astype(jnp.float32), axis=0)
    return output, d_hidden, summed.astype(jnp.bfloat16)[None]


def solution(mesh):
    in_specs = (
        P(("dp", "expert"), None),
        P(("dp", "expert"), "tensor"),
        P("expert", None, "tensor"),
        P(("dp", "expert"), None),
        P(),
    )
    out_specs = (
        P(("dp", "expert"), "tensor"),
        P(("dp", "expert"), "tensor"),
        P("expert", "dp", "tensor"),
    )
    small = mesh.shape["dp"] == 2 and mesh.shape["expert"] == 4 and mesh.shape["tensor"] in (2, 4)
    shards = few if small else many
    return jax.shard_map(shards, mesh=mesh, in_specs=in_specs, out_specs=out_specs, check_vma=False)
```

```python
import functools

import jax
import jax.numpy as jnp
from jax import lax
from jax.experimental import pallas as pl
from jax.experimental.pallas import tpu as pltpu
from jax.sharding import PartitionSpec as P

VMEM = pl.BlockSpec(memory_space=pltpu.VMEM)
ANY = pl.BlockSpec(memory_space=pl.ANY)


def call(kernel, outs, ins, specs=None, scratch=(), after=(), out_specs=None):
    name = getattr(kernel, "func", kernel).__name__

    def late(*refs):
        kernel(*refs[: len(ins)], *refs[len(ins) + len(after) :])

    return pl.pallas_call(
        late,
        out_shape=tuple(jax.ShapeDtypeStruct(s, d) for s, d in outs),
        in_specs=[*(specs or [VMEM] * len(ins)), *[ANY] * len(after)],
        out_specs=tuple(out_specs or [VMEM] * len(outs)),
        scratch_shapes=list(scratch),
        name=name,
        cost_estimate=pl.CostEstimate(flops=1000, bytes_accessed=1000, transcendentals=0),
        compiler_params=pltpu.CompilerParams(vmem_limit_bytes=24 << 20),
    )(*ins, *after)


def far(value):
    return pltpu.with_memory_space_constraint(value, pltpu.HBM)


def swap(value, axis, offset):
    size = lax.axis_size(axis)
    return lax.ppermute(value, axis, [(i, i ^ offset) for i in range(size)])


def route(routes, placement, experts, cap):
    chosen = routes == jnp.arange(placement.shape[0], dtype=jnp.int32)[None, :]
    target = jnp.sum(jnp.where(chosen, placement[None, :], 0), axis=1)
    landing = target[:, None] == jnp.arange(experts, dtype=jnp.int32)[None, :]
    counted = jnp.cumsum(landing.astype(jnp.int32), axis=0) - 1
    within = jnp.sum(jnp.where(landing, counted, 0), axis=1)
    return target, within


def slot_of(routes, placement, owner, experts, cap):
    tok = routes.shape[1]
    target = jnp.zeros((1, tok), jnp.int32)
    for j in range(experts):
        target = jnp.where(routes == j, placement[j : j + 1, :tok], target)
    key = jnp.bitwise_xor(target, owner)
    landing = jnp.where(key == lax.broadcasted_iota(jnp.int32, (max(8, experts), tok), 0), 1.0, 0.0)
    earlier = lax.broadcasted_iota(jnp.int32, (tok, tok), 0) <= lax.broadcasted_iota(jnp.int32, (tok, tok), 1)
    counted = jnp.dot(
        landing.astype(jnp.bfloat16),
        jnp.where(earlier, 1.0, 0.0).astype(jnp.bfloat16),
        preferred_element_type=jnp.float32,
    )
    within = jnp.sum(landing * counted, axis=0, keepdims=True).astype(jnp.int32) - 1
    position = key * cap + within
    slots = lax.broadcasted_iota(jnp.int32, (experts * cap, tok), 0)
    return jnp.where(position == slots, 1.0, 0.0).astype(jnp.bfloat16)


def chosen(slot, value):
    return jnp.dot(slot, value, preferred_element_type=jnp.float32).astype(jnp.bfloat16)


def pick_own(cap, routes, placement, grad, hid, slot_out, near_g, near_h, far_g, far_h, table, *refs):
    routes_held, placement_held, grad_held, hid_held, sem = refs
    copies = [
        pltpu.make_async_copy(*pair, sem.at[i])
        for i, pair in enumerate(
            ((routes, routes_held), (placement, placement_held), (grad, grad_held), (hid, hid_held))
        )
    ]
    for copy in copies:
        copy.start()
    copies[0].wait()
    copies[1].wait()
    experts = placement.shape[0]
    for j in range(experts):
        table[j : j + 1] = jnp.full((1, table.shape[1]), placement_held[j], jnp.int32)
    slot = slot_of(routes_held[...], table, lax.axis_index("expert"), experts, cap)
    slot_out[...] = slot
    near, far_slots = slot[:cap], slot[2 * cap : 3 * cap]
    copies[2].wait()
    far_g[...] = chosen(far_slots, grad_held[...])
    near_g[...] = chosen(near, grad_held[...])
    copies[3].wait()
    far_h[...] = chosen(far_slots, hid_held[...])
    near_h[...] = chosen(near, hid_held[...])


def pick_next(cap, *refs):
    table, routes, grad, hid, own_near_g, own_near_h, own_far_g, own_far_h = refs[:8]
    near_g, near_h, far_g, far_h, near_pack = refs[8:]
    slot = slot_of(routes[...], table, jnp.bitwise_xor(lax.axis_index("expert"), 1), lax.axis_size("expert"), cap)
    near, far_slots = slot[cap : 2 * cap], slot[3 * cap :]
    for own, rows, value, out in (
        (own_far_g, far_slots, grad, far_g),
        (own_near_g, near, grad, near_g),
        (own_near_h, near, hid, near_h),
        (own_far_h, far_slots, hid, far_h),
    ):
        out[:cap] = own[...]
        out[cap:] = chosen(rows, value[...])
    cols, share = near_g.shape[1], near_h.shape[1] // 2
    near_pack[:, :cols] = near_g[...]
    near_pack[:, cols:] = near_h[:, other_share(share)]


def own_share(share):
    return pl.ds(pl.multiple_of(lax.axis_index("dp") * share, share), share)


def other_share(share):
    return pl.ds(pl.multiple_of((1 - lax.axis_index("dp")) * share, share), share)


def cut_other(hid, out):
    out[...] = hid[:, other_share(out.shape[1])]


def hidden_grad(weight, i, grads, out):
    rows = weight.shape[1]
    part = lax.dot_general(grads[...], weight[i], (((1,), (1,)), ((), ())), preferred_element_type=jnp.float32)
    out[:, i * rows : (i + 1) * rows] = part.astype(out.dtype)


def output_rows(first, weight, hids, total):
    blocks, rows, _ = weight.shape
    for i in range(blocks):
        block = jnp.bitwise_xor(lax.axis_index("tensor"), first + 2 * i)
        start = pl.multiple_of(block * rows, rows)
        term = jnp.dot(hids[:, pl.ds(start, rows)], weight[i], preferred_element_type=jnp.float32)
        total = term if total is None else total + term
    return total


def weight_copies(first, weight, held, sem):
    rows = held.shape[1]
    copies = []
    for i in range(held.shape[0]):
        block = jnp.bitwise_xor(lax.axis_index("tensor"), first + 2 * i)
        start = pl.multiple_of(block * rows, rows)
        copies.append(pltpu.make_async_copy(weight.at[0, pl.ds(start, rows)], held.at[i], sem.at[i]))
        copies[i].start()
    return copies


def near_odd(weight, grads, odd, send, sem):
    for i, copy in enumerate(weight_copies(1, weight, odd, sem)):
        copy.wait()
        hidden_grad(odd, i, grads, send)


def near_even(weight, odd, grads, hids, even, keep, own, following, sem):
    copies = weight_copies(0, weight, even, sem)
    total = output_rows(1, odd, hids, None)
    for i, copy in enumerate(copies):
        copy.wait()
        hidden_grad(even, i, grads, keep)
    cut_rows(output_rows(0, even, hids, total), (own, following))


def cut_rows(total, outs):
    rows = min(outs[0].shape[0], total.shape[0])
    for i, out in enumerate(outs):
        out[:rows] = total[i * rows : (i + 1) * rows].astype(out.dtype)
        if out.shape[0] > rows:
            out[rows:] = jnp.zeros((out.shape[0] - rows, out.shape[1]), out.dtype)


def far_grads(weight, grads, out):
    for i in range(weight.shape[0]):
        hidden_grad(weight, i, grads, out)


def far_outs(odd, even, hids, *outs):
    cut_rows(output_rows(0, even, hids, output_rows(1, odd, hids, None)), outs)


def fold(keep, got, *outs):
    total = keep[...] + got[...].astype(jnp.float32)
    if outs[0].dtype == jnp.float32:
        cut = outs[0].shape[1]
        outs[0][...] = total[:, :cut]
        outs[1][...] = total[:, cut:].astype(outs[1].dtype)
    else:
        cut_rows(total, outs)


def place(cap, slot, *refs):
    *rows, out, token = refs
    rows = [ref[...] if ref.shape[0] == cap else ref[i % 2 * cap : (i % 2 + 1) * cap] for i, ref in enumerate(rows)]
    out[...] = lax.dot_general(
        slot[...], jnp.concatenate(rows, axis=0), (((0,), (0,)), ((), ())), preferred_element_type=jnp.float32
    ).astype(out.dtype)
    token[...] = jnp.zeros_like(token)


def outer_near(grads, hids, both, far_grads, far_hids, out):
    cols, share = grads.shape[1], out.shape[0]
    part = own_share(share)
    g = jnp.concatenate([grads[...], both[:, :cols], far_grads[...]], axis=0)
    h = jnp.concatenate([hids[:, part], both[:, cols:], far_hids[:, part]], axis=0)
    out[...] = lax.dot_general(h, g, (((0,), (0,)), ((), ())), preferred_element_type=jnp.float32)


def outer_far(near, grads, hids, out, token, held, sem):
    pieces, rows, _ = held.shape
    copies = []
    for i in range(pieces):
        part = slice(i * rows, (i + 1) * rows)
        term = lax.dot_general(
            hids[:, part], grads[...], (((0,), (0,)), ((), ())), preferred_element_type=jnp.float32
        )
        held[i] = (near[part] + term).astype(held.dtype)
        copies.append(pltpu.make_async_copy(held.at[i], out.at[0, pl.ds(i * rows, rows)], sem.at[i]))
        copies[i].start()
    token[...] = jnp.zeros_like(token)
    for copy in copies:
        copy.wait()


def few(hidden, out_grad, w_down, routes, placement):
    experts = lax.axis_size("expert")
    tensors = lax.axis_size("tensor")
    tok, width = hidden.shape
    cols = out_grad.shape[1]
    cap = 2 * tok // experts
    slots = experts * cap
    share = width // 2
    column = width // tensors
    bf, f32 = jnp.bfloat16, jnp.float32
    rows = 2 * cap
    kept, cut, token = (rows, width // 2), (rows, column), ((8, 128), f32)
    pair = ((cap, column), bf)

    routes = routes.reshape(1, tok)
    next_routes, next_grad, next_hid = (swap(x, "expert", 1) for x in (routes, out_grad, hidden))
    slot, near_g, near_h, far_g, far_h, table = call(
        functools.partial(pick_own, cap),
        [((slots, tok), bf), *[((cap, cols), bf), ((cap, width), bf)] * 2, ((8, 128), jnp.int32)],
        tuple(far(x) for x in (routes, placement, out_grad, hidden)),
        [ANY] * 4,
        [
            pltpu.VMEM((1, tok), jnp.int32),
            pltpu.SMEM((experts,), jnp.int32),
            pltpu.VMEM((tok, cols), bf),
            pltpu.VMEM((tok, width), bf),
            pltpu.SemaphoreType.DMA((4,)),
        ],
    )
    near_g, near_h, far_g, far_h, near_pack = call(
        functools.partial(pick_next, cap),
        [*[((rows, cols), bf), ((rows, width), bf)] * 2, ((rows, cols + share), bf)],
        (table, next_routes, next_grad, next_hid, near_g, near_h, far_g, far_h),
    )
    far_h = swap(far_h, "expert", 2)
    far_g = swap(far_g, "expert", 2)
    other_near = swap(near_pack, "dp", 1)
    part = ((tensors // 2, column, cols), bf)
    sems = [pltpu.SemaphoreType.DMA((tensors // 2,))]
    odd, near_send = call(
        near_odd, [part, (kept, bf)], (far(w_down), near_g), [ANY, VMEM], sems
    )
    near_got = swap(near_send, "tensor", 1)
    even, near_keep, near_out, next_out = call(
        near_even,
        [part, (kept, f32), ((cap, cols), bf), ((cap, cols), bf)],
        (far(w_down), odd, near_g, near_h),
        [ANY, *[VMEM] * 3],
        sems,
    )
    next_out = swap(next_out, "expert", 1)
    (far_send,) = call(far_grads, [(kept, bf)], (odd, far_g), after=(near_keep,))
    far_got = swap(far_send, "tensor", 1)
    (far_keep,) = call(far_grads, [(kept, f32)], (even, far_g), after=(far_send,))
    other_g = swap(far_g, "dp", 1)
    last = far_keep
    if tensors > 2:
        near_keep, near_send = call(fold, [(cut, f32), (cut, bf)], (near_keep, near_got), after=(last,))
        near_got = swap(near_send, "tensor", 2)
        last = near_send
    far_out = call(far_outs, [((cap, cols), bf)] * 2, (odd, even, far_h), after=(last, next_out))
    last = far_out[0]
    if tensors > 2:
        far_keep, far_send = call(fold, [(cut, f32), (cut, bf)], (far_keep, far_got), after=(last, other_near))
        far_got = swap(far_send, "tensor", 2)
        last = far_send
    (cut_h,) = call(cut_other, [((rows, share), bf)], (far_h,), after=(last,))
    other_h = swap(cut_h, "dp", 1)
    (near_total,) = call(outer_near, [((share, cols), f32)], (near_g, near_h, other_near, far_g, far_h), after=(cut_h,))
    (near_back,) = call(fold, [((rows + 16, column), bf)], (near_keep, near_got), after=(near_total,))
    next_back = swap(near_back, "expert", 1)
    far_back = call(fold, [pair, pair], (far_keep, far_got), after=(near_back, other_g))
    output, last = call(
        functools.partial(place, cap),
        [((tok, cols), bf), token],
        (slot, near_out, next_out, swap(far_out[0], "expert", 2), swap(far_out[1], "expert", 3)),
        after=(far_back[0],),
    )
    pieces = 8
    d_weight, last = call(
        outer_far,
        [((1, share, cols), bf), token],
        (near_total, other_g, other_h),
        None,
        [pltpu.VMEM((pieces, share // pieces, cols), bf), pltpu.SemaphoreType.DMA((pieces,))],
        after=(last,),
        out_specs=[ANY, VMEM],
    )
    d_hidden, _ = call(
        functools.partial(place, cap),
        [((tok, column), bf), token],
        (
            slot,
            near_back,
            next_back,
            swap(far_back[0], "expert", 2),
            swap(far_back[1], "expert", 3),
        ),
        after=(last,),
    )
    return output, d_hidden, d_weight


def many(hidden, out_grad, w_down, routes, placement):
    experts = lax.axis_size("expert")
    tok = hidden.shape[0]
    width = hidden.shape[1]
    cols = out_grad.shape[1]
    cap = 2 * tok // experts
    slots = experts * cap
    target, within = route(routes, placement, experts, cap)
    position = target * cap + within
    picker = (jnp.arange(slots, dtype=jnp.int32)[:, None] == position[None, :]).astype(jnp.bfloat16)
    send_hidden = jnp.dot(picker, hidden, preferred_element_type=jnp.float32).astype(jnp.bfloat16)
    send_grad = jnp.dot(picker, out_grad, preferred_element_type=jnp.float32).astype(jnp.bfloat16)

    def exchange(value):
        return lax.all_to_all(
            value.reshape(experts, cap, -1), "expert", split_axis=0, concat_axis=0, tiled=True
        ).reshape(slots, -1)

    slot_hidden, slot_grad = exchange(send_hidden), exchange(send_grad)
    weight = w_down[0]
    out_rows = jnp.dot(slot_hidden, weight, preferred_element_type=jnp.float32).astype(jnp.bfloat16)
    partial_value = lax.dot_general(
        slot_grad, weight, (((1,), (1,)), ((), ())), preferred_element_type=jnp.float32
    )
    hidden_grad = lax.psum_scatter(partial_value, "tensor", scatter_dimension=1, tiled=True).astype(
        jnp.bfloat16
    )

    def place(rows):
        return jnp.einsum("rt,rd->td", picker, rows, preferred_element_type=jnp.float32).astype(jnp.bfloat16)

    output, d_hidden = place(exchange(out_rows)), place(exchange(hidden_grad))
    share = width // lax.axis_size("dp")
    mine = lax.axis_index("dp") * share
    part_h = lax.dynamic_slice_in_dim(
        lax.all_gather(slot_hidden, "dp", axis=0, tiled=True), mine, share, 1
    ).reshape(-1, slots, share)
    part_g = lax.all_gather(slot_grad, "dp", axis=0, tiled=True).reshape(-1, slots, cols)
    terms = jnp.einsum("krf,krd->kfd", part_h, part_g, preferred_element_type=jnp.float32)
    rounded = lax.optimization_barrier(terms.astype(jnp.bfloat16))
    summed = jnp.sum(rounded.astype(jnp.float32), axis=0)
    return output, d_hidden, summed.astype(jnp.bfloat16)[None]


def solution(mesh):
    in_specs = (
        P(("dp", "expert"), None),
        P(("dp", "expert"), "tensor"),
        P("expert", None, "tensor"),
        P(("dp", "expert"), None),
        P(),
    )
    out_specs = (
        P(("dp", "expert"), "tensor"),
        P(("dp", "expert"), "tensor"),
        P("expert", "dp", "tensor"),
    )
    small = mesh.shape["dp"] == 2 and mesh.shape["expert"] == 4 and mesh.shape["tensor"] in (2, 4)
    shards = few if small else many
    return jax.shard_map(shards, mesh=mesh, in_specs=in_specs, out_specs=out_specs, check_vma=False)
```

```python
import functools

import jax
import jax.numpy as jnp
from jax import lax
from jax.experimental import pallas as pl
from jax.experimental.pallas import tpu as pltpu
from jax.sharding import PartitionSpec as P

VMEM = pl.BlockSpec(memory_space=pltpu.VMEM)
ANY = pl.BlockSpec(memory_space=pl.ANY)


def call(kernel, outs, ins, specs=None, scratch=(), after=(), out_specs=None):
    name = getattr(kernel, "func", kernel).__name__

    def late(*refs):
        kernel(*refs[: len(ins)], *refs[len(ins) + len(after) :])

    return pl.pallas_call(
        late,
        out_shape=tuple(jax.ShapeDtypeStruct(s, d) for s, d in outs),
        in_specs=[*(specs or [VMEM] * len(ins)), *[ANY] * len(after)],
        out_specs=tuple(out_specs or [VMEM] * len(outs)),
        scratch_shapes=list(scratch),
        name=name,
        cost_estimate=pl.CostEstimate(flops=1000, bytes_accessed=1000, transcendentals=0),
        compiler_params=pltpu.CompilerParams(vmem_limit_bytes=24 << 20),
    )(*ins, *after)


def far(value):
    return pltpu.with_memory_space_constraint(value, pltpu.HBM)


def swap(value, axis, offset):
    size = lax.axis_size(axis)
    return lax.ppermute(value, axis, [(i, i ^ offset) for i in range(size)])


def route(routes, placement, experts, cap):
    chosen = routes == jnp.arange(placement.shape[0], dtype=jnp.int32)[None, :]
    target = jnp.sum(jnp.where(chosen, placement[None, :], 0), axis=1)
    landing = target[:, None] == jnp.arange(experts, dtype=jnp.int32)[None, :]
    counted = jnp.cumsum(landing.astype(jnp.int32), axis=0) - 1
    within = jnp.sum(jnp.where(landing, counted, 0), axis=1)
    return target, within


def slot_of(routes, placement, owner, experts, cap):
    tok = routes.shape[1]
    target = jnp.zeros((1, tok), jnp.int32)
    for j in range(experts):
        target = jnp.where(routes == j, placement[j : j + 1, :tok], target)
    key = jnp.bitwise_xor(target, owner)
    landing = jnp.where(key == lax.broadcasted_iota(jnp.int32, (max(8, experts), tok), 0), 1.0, 0.0)
    earlier = lax.broadcasted_iota(jnp.int32, (tok, tok), 0) <= lax.broadcasted_iota(jnp.int32, (tok, tok), 1)
    counted = jnp.dot(
        landing.astype(jnp.bfloat16),
        jnp.where(earlier, 1.0, 0.0).astype(jnp.bfloat16),
        preferred_element_type=jnp.float32,
    )
    within = jnp.sum(landing * counted, axis=0, keepdims=True).astype(jnp.int32) - 1
    position = key * cap + within
    slots = lax.broadcasted_iota(jnp.int32, (experts * cap, tok), 0)
    return jnp.where(position == slots, 1.0, 0.0).astype(jnp.bfloat16)


def chosen(slot, value):
    return jnp.dot(slot, value, preferred_element_type=jnp.float32).astype(jnp.bfloat16)


def pick_own(cap, routes, placement, grad, hid, slot_out, table, grad_out, hid_out, far_g, *refs):
    routes_held, placement_held, sem = refs
    copies = [
        pltpu.make_async_copy(*pair, sem.at[i])
        for i, pair in enumerate(
            ((routes, routes_held), (placement, placement_held), (grad, grad_out), (hid, hid_out))
        )
    ]
    for copy in copies:
        copy.start()
    copies[0].wait()
    copies[1].wait()
    experts = placement.shape[0]
    for j in range(experts):
        table[j : j + 1] = jnp.full((1, table.shape[1]), placement_held[j], jnp.int32)
    slot = slot_of(routes_held[...], table, lax.axis_index("expert"), experts, cap)
    slot_out[...] = slot
    copies[2].wait()
    far_g[...] = chosen(slot[2 * cap : 3 * cap], grad_out[...])
    copies[3].wait()


def pick_next(cap, table, routes, grad, own_far_g, slot_out, far_g):
    experts = lax.axis_size("expert")
    slot = slot_of(routes[...], table, jnp.bitwise_xor(lax.axis_index("expert"), 1), experts, cap)
    slot_out[...] = slot
    far_g[:cap] = own_far_g[...]
    far_g[cap:] = chosen(slot[3 * cap :], grad[...])


def pick_rest(cap, slot, next_slot, grad, hid, next_grad, next_hid, near_g, near_h, far_h, near_pack):
    for own, other, value, next_value, out in (
        (0, 1, grad, next_grad, near_g),
        (0, 1, hid, next_hid, near_h),
        (2, 3, hid, next_hid, far_h),
    ):
        out[:cap] = chosen(slot[own * cap : (own + 1) * cap], value[...])
        out[cap:] = chosen(next_slot[other * cap : (other + 1) * cap], next_value[...])
    cols, share = near_g.shape[1], near_h.shape[1] // 2
    near_pack[:, :cols] = near_g[...]
    near_pack[:, cols:] = near_h[:, other_share(share)]


def own_share(share):
    return pl.ds(pl.multiple_of(lax.axis_index("dp") * share, share), share)


def other_share(share):
    return pl.ds(pl.multiple_of((1 - lax.axis_index("dp")) * share, share), share)


def cut_other(hid, out):
    out[...] = hid[:, other_share(out.shape[1])]


def hidden_grad(weight, i, grads, out):
    rows = weight.shape[1]
    part = lax.dot_general(grads[...], weight[i], (((1,), (1,)), ((), ())), preferred_element_type=jnp.float32)
    out[:, i * rows : (i + 1) * rows] = part.astype(out.dtype)


def output_rows(first, weight, hids, total):
    blocks, rows, _ = weight.shape
    for i in range(blocks):
        block = jnp.bitwise_xor(lax.axis_index("tensor"), first + 2 * i)
        start = pl.multiple_of(block * rows, rows)
        term = jnp.dot(hids[:, pl.ds(start, rows)], weight[i], preferred_element_type=jnp.float32)
        total = term if total is None else total + term
    return total


def weight_copies(first, weight, held, sem):
    rows = held.shape[1]
    copies = []
    for i in range(held.shape[0]):
        block = jnp.bitwise_xor(lax.axis_index("tensor"), first + 2 * i)
        start = pl.multiple_of(block * rows, rows)
        copies.append(pltpu.make_async_copy(weight.at[0, pl.ds(start, rows)], held.at[i], sem.at[i]))
        copies[i].start()
    return copies


def near_odd(weight, grads, odd, send, sem):
    for i, copy in enumerate(weight_copies(1, weight, odd, sem)):
        copy.wait()
        hidden_grad(odd, i, grads, send)


def near_even(weight, odd, grads, hids, even, keep, own, following, sem):
    copies = weight_copies(0, weight, even, sem)
    total = output_rows(1, odd, hids, None)
    for i, copy in enumerate(copies):
        copy.wait()
        hidden_grad(even, i, grads, keep)
    cut_rows(output_rows(0, even, hids, total), (own, following))


def cut_rows(total, outs):
    rows = min(outs[0].shape[0], total.shape[0])
    for i, out in enumerate(outs):
        out[:rows] = total[i * rows : (i + 1) * rows].astype(out.dtype)
        if out.shape[0] > rows:
            out[rows:] = jnp.zeros((out.shape[0] - rows, out.shape[1]), out.dtype)


def far_grads(weight, grads, out):
    for i in range(weight.shape[0]):
        hidden_grad(weight, i, grads, out)


def far_outs(odd, even, hids, *outs):
    cut_rows(output_rows(0, even, hids, output_rows(1, odd, hids, None)), outs)


def fold(keep, got, *outs):
    total = keep[...] + got[...].astype(jnp.float32)
    if outs[0].dtype == jnp.float32:
        cut = outs[0].shape[1]
        outs[0][...] = total[:, :cut]
        outs[1][...] = total[:, cut:].astype(outs[1].dtype)
    else:
        cut_rows(total, outs)


def place(cap, slot, *refs):
    *rows, out, token = refs
    rows = [ref[...] if ref.shape[0] == cap else ref[i % 2 * cap : (i % 2 + 1) * cap] for i, ref in enumerate(rows)]
    out[...] = lax.dot_general(
        slot[...], jnp.concatenate(rows, axis=0), (((0,), (0,)), ((), ())), preferred_element_type=jnp.float32
    ).astype(out.dtype)
    token[...] = jnp.zeros_like(token)


def outer_near(grads, hids, both, far_grads, far_hids, out):
    cols, share = grads.shape[1], out.shape[0]
    part = own_share(share)
    g = jnp.concatenate([grads[...], both[:, :cols], far_grads[...]], axis=0)
    h = jnp.concatenate([hids[:, part], both[:, cols:], far_hids[:, part]], axis=0)
    out[...] = lax.dot_general(h, g, (((0,), (0,)), ((), ())), preferred_element_type=jnp.float32)


def outer_far(near, grads, hids, out, token, held, sem):
    pieces, rows, _ = held.shape
    copies = []
    for i in range(pieces):
        part = slice(i * rows, (i + 1) * rows)
        term = lax.dot_general(
            hids[:, part], grads[...], (((0,), (0,)), ((), ())), preferred_element_type=jnp.float32
        )
        held[i] = (near[part] + term).astype(held.dtype)
        copies.append(pltpu.make_async_copy(held.at[i], out.at[0, pl.ds(i * rows, rows)], sem.at[i]))
        copies[i].start()
    token[...] = jnp.zeros_like(token)
    for copy in copies:
        copy.wait()


def few(hidden, out_grad, w_down, routes, placement):
    experts = lax.axis_size("expert")
    tensors = lax.axis_size("tensor")
    tok, width = hidden.shape
    cols = out_grad.shape[1]
    cap = 2 * tok // experts
    slots = experts * cap
    share = width // 2
    column = width // tensors
    bf, f32 = jnp.bfloat16, jnp.float32
    rows = 2 * cap
    kept, cut, token = (rows, width // 2), (rows, column), ((8, 128), f32)
    pair = ((cap, column), bf)

    routes = routes.reshape(1, tok)
    next_routes, next_grad, next_hid = (swap(x, "expert", 1) for x in (routes, out_grad, hidden))
    slot, table, grad, hid, far_g = call(
        functools.partial(pick_own, cap),
        [((slots, tok), bf), ((8, 128), jnp.int32), ((tok, cols), bf), ((tok, width), bf), ((cap, cols), bf)],
        tuple(far(x) for x in (routes, placement, out_grad, hidden)),
        [ANY] * 4,
        [
            pltpu.VMEM((1, tok), jnp.int32),
            pltpu.SMEM((experts,), jnp.int32),
            pltpu.SemaphoreType.DMA((4,)),
        ],
    )
    next_slot, far_g = call(
        functools.partial(pick_next, cap),
        [((slots, tok), bf), ((rows, cols), bf)],
        (table, next_routes, next_grad, far_g),
    )
    near_g, near_h, far_h, near_pack = call(
        functools.partial(pick_rest, cap),
        [((rows, cols), bf), ((rows, width), bf), ((rows, width), bf), ((rows, cols + share), bf)],
        (slot, next_slot, grad, hid, next_grad, next_hid),
    )
    far_h = swap(far_h, "expert", 2)
    far_g = swap(far_g, "expert", 2)
    other_near = swap(near_pack, "dp", 1)
    part = ((tensors // 2, column, cols), bf)
    sems = [pltpu.SemaphoreType.DMA((tensors // 2,))]
    odd, near_send = call(
        near_odd, [part, (kept, bf)], (far(w_down), near_g), [ANY, VMEM], sems
    )
    near_got = swap(near_send, "tensor", 1)
    even, near_keep, near_out, next_out = call(
        near_even,
        [part, (kept, f32), ((cap, cols), bf), ((cap, cols), bf)],
        (far(w_down), odd, near_g, near_h),
        [ANY, *[VMEM] * 3],
        sems,
    )
    next_out = swap(next_out, "expert", 1)
    (far_send,) = call(far_grads, [(kept, bf)], (odd, far_g), after=(near_keep,))
    far_got = swap(far_send, "tensor", 1)
    other_g = swap(far_g, "dp", 1)
    last = far_send
    if tensors > 2:
        near_keep, near_send = call(fold, [(cut, f32), (cut, bf)], (near_keep, near_got), after=(last,))
        near_got = swap(near_send, "tensor", 2)
        last = near_send
    (far_keep,) = call(far_grads, [(kept, f32)], (even, far_g), after=(last,))
    last = far_keep
    far_out = call(far_outs, [((cap, cols), bf)] * 2, (odd, even, far_h), after=(last, next_out))
    last = far_out[0]
    if tensors > 2:
        far_keep, far_send = call(fold, [(cut, f32), (cut, bf)], (far_keep, far_got), after=(last, other_near))
        far_got = swap(far_send, "tensor", 2)
        last = far_send
    (cut_h,) = call(cut_other, [((rows, share), bf)], (far_h,), after=(last,))
    other_h = swap(cut_h, "dp", 1)
    (near_total,) = call(outer_near, [((share, cols), f32)], (near_g, near_h, other_near, far_g, far_h), after=(cut_h,))
    (near_back,) = call(fold, [((rows + 16, column), bf)], (near_keep, near_got), after=(near_total,))
    next_back = swap(near_back, "expert", 1)
    back = [swap(far_out[k], "expert", 2 + k) for k in (1, 0)]
    far_back = call(fold, [pair, pair], (far_keep, far_got), after=(near_back, other_g))
    output, last = call(
        functools.partial(place, cap),
        [((tok, cols), bf), token],
        (slot, near_out, next_out, back[1], back[0]),
        after=(far_back[0],),
    )
    pieces = 8
    d_weight, last = call(
        outer_far,
        [((1, share, cols), bf), token],
        (near_total, other_g, other_h),
        None,
        [pltpu.VMEM((pieces, share // pieces, cols), bf), pltpu.SemaphoreType.DMA((pieces,))],
        after=(last,),
        out_specs=[ANY, VMEM],
    )
    d_hidden, _ = call(
        functools.partial(place, cap),
        [((tok, column), bf), token],
        (
            slot,
            near_back,
            next_back,
            swap(far_back[0], "expert", 2),
            swap(far_back[1], "expert", 3),
        ),
        after=(last,),
    )
    return output, d_hidden, d_weight


def many(hidden, out_grad, w_down, routes, placement):
    experts = lax.axis_size("expert")
    tok = hidden.shape[0]
    width = hidden.shape[1]
    cols = out_grad.shape[1]
    cap = 2 * tok // experts
    slots = experts * cap
    target, within = route(routes, placement, experts, cap)
    position = target * cap + within
    picker = (jnp.arange(slots, dtype=jnp.int32)[:, None] == position[None, :]).astype(jnp.bfloat16)
    send_hidden = jnp.dot(picker, hidden, preferred_element_type=jnp.float32).astype(jnp.bfloat16)
    send_grad = jnp.dot(picker, out_grad, preferred_element_type=jnp.float32).astype(jnp.bfloat16)

    def exchange(value):
        return lax.all_to_all(
            value.reshape(experts, cap, -1), "expert", split_axis=0, concat_axis=0, tiled=True
        ).reshape(slots, -1)

    slot_hidden, slot_grad = exchange(send_hidden), exchange(send_grad)
    weight = w_down[0]
    out_rows = jnp.dot(slot_hidden, weight, preferred_element_type=jnp.float32).astype(jnp.bfloat16)
    partial_value = lax.dot_general(
        slot_grad, weight, (((1,), (1,)), ((), ())), preferred_element_type=jnp.float32
    )
    hidden_grad = lax.psum_scatter(partial_value, "tensor", scatter_dimension=1, tiled=True).astype(
        jnp.bfloat16
    )

    def place(rows):
        return jnp.einsum("rt,rd->td", picker, rows, preferred_element_type=jnp.float32).astype(jnp.bfloat16)

    output, d_hidden = place(exchange(out_rows)), place(exchange(hidden_grad))
    share = width // lax.axis_size("dp")
    mine = lax.axis_index("dp") * share
    part_h = lax.dynamic_slice_in_dim(
        lax.all_gather(slot_hidden, "dp", axis=0, tiled=True), mine, share, 1
    ).reshape(-1, slots, share)
    part_g = lax.all_gather(slot_grad, "dp", axis=0, tiled=True).reshape(-1, slots, cols)
    terms = jnp.einsum("krf,krd->kfd", part_h, part_g, preferred_element_type=jnp.float32)
    rounded = lax.optimization_barrier(terms.astype(jnp.bfloat16))
    summed = jnp.sum(rounded.astype(jnp.float32), axis=0)
    return output, d_hidden, summed.astype(jnp.bfloat16)[None]


def solution(mesh):
    in_specs = (
        P(("dp", "expert"), None),
        P(("dp", "expert"), "tensor"),
        P("expert", None, "tensor"),
        P(("dp", "expert"), None),
        P(),
    )
    out_specs = (
        P(("dp", "expert"), "tensor"),
        P(("dp", "expert"), "tensor"),
        P("expert", "dp", "tensor"),
    )
    small = mesh.shape["dp"] == 2 and mesh.shape["expert"] == 4 and mesh.shape["tensor"] in (2, 4)
    shards = few if small else many
    return jax.shard_map(shards, mesh=mesh, in_specs=in_specs, out_specs=out_specs, check_vma=False)
```

```python
import functools

import jax
import jax.numpy as jnp
from jax import lax
from jax.experimental import pallas as pl
from jax.experimental.pallas import tpu as pltpu
from jax.sharding import PartitionSpec as P

VMEM = pl.BlockSpec(memory_space=pltpu.VMEM)
ANY = pl.BlockSpec(memory_space=pl.ANY)


def call(kernel, outs, ins, specs=None, scratch=(), after=(), out_specs=None):
    name = getattr(kernel, "func", kernel).__name__

    def late(*refs):
        kernel(*refs[: len(ins)], *refs[len(ins) + len(after) :])

    return pl.pallas_call(
        late,
        out_shape=tuple(jax.ShapeDtypeStruct(s, d) for s, d in outs),
        in_specs=[*(specs or [VMEM] * len(ins)), *[ANY] * len(after)],
        out_specs=tuple(out_specs or [VMEM] * len(outs)),
        scratch_shapes=list(scratch),
        name=name,
        cost_estimate=pl.CostEstimate(flops=1000, bytes_accessed=1000, transcendentals=0),
        compiler_params=pltpu.CompilerParams(vmem_limit_bytes=24 << 20),
    )(*ins, *after)


def far(value):
    return pltpu.with_memory_space_constraint(value, pltpu.HBM)


def swap(value, axis, offset):
    size = lax.axis_size(axis)
    return lax.ppermute(value, axis, [(i, i ^ offset) for i in range(size)])


def route(routes, placement, experts, cap):
    chosen = routes == jnp.arange(placement.shape[0], dtype=jnp.int32)[None, :]
    target = jnp.sum(jnp.where(chosen, placement[None, :], 0), axis=1)
    landing = target[:, None] == jnp.arange(experts, dtype=jnp.int32)[None, :]
    counted = jnp.cumsum(landing.astype(jnp.int32), axis=0) - 1
    within = jnp.sum(jnp.where(landing, counted, 0), axis=1)
    return target, within


def slot_of(routes, placement, owner, experts, cap):
    tok = routes.shape[1]
    target = jnp.zeros((1, tok), jnp.int32)
    for j in range(experts):
        target = jnp.where(routes == j, placement[j : j + 1, :tok], target)
    key = jnp.bitwise_xor(target, owner)
    landing = jnp.where(key == lax.broadcasted_iota(jnp.int32, (max(8, experts), tok), 0), 1.0, 0.0)
    earlier = lax.broadcasted_iota(jnp.int32, (tok, tok), 0) <= lax.broadcasted_iota(jnp.int32, (tok, tok), 1)
    counted = jnp.dot(
        landing.astype(jnp.bfloat16),
        jnp.where(earlier, 1.0, 0.0).astype(jnp.bfloat16),
        preferred_element_type=jnp.float32,
    )
    within = jnp.sum(landing * counted, axis=0, keepdims=True).astype(jnp.int32) - 1
    position = key * cap + within
    slots = lax.broadcasted_iota(jnp.int32, (experts * cap, tok), 0)
    return jnp.where(position == slots, 1.0, 0.0).astype(jnp.bfloat16)


def chosen(slot, value):
    return jnp.dot(slot, value, preferred_element_type=jnp.float32).astype(jnp.bfloat16)


def pick_own(cap, routes, placement, grad, hid, slot_out, table, grad_out, hid_out, far_g, *refs):
    routes_held, placement_held, sem = refs
    copies = [
        pltpu.make_async_copy(*pair, sem.at[i])
        for i, pair in enumerate(
            ((routes, routes_held), (placement, placement_held), (grad, grad_out), (hid, hid_out))
        )
    ]
    for copy in copies:
        copy.start()
    copies[0].wait()
    copies[1].wait()
    experts = placement.shape[0]
    for j in range(experts):
        table[j : j + 1] = jnp.full((1, table.shape[1]), placement_held[j], jnp.int32)
    slot = slot_of(routes_held[...], table, lax.axis_index("expert"), experts, cap)
    slot_out[...] = slot
    copies[2].wait()
    far_g[...] = chosen(slot[2 * cap : 3 * cap], grad_out[...])
    copies[3].wait()


def pick_next(cap, table, routes, grad, own_far_g, slot_out, far_g):
    experts = lax.axis_size("expert")
    slot = slot_of(routes[...], table, jnp.bitwise_xor(lax.axis_index("expert"), 1), experts, cap)
    slot_out[...] = slot
    far_g[:cap] = own_far_g[...]
    far_g[cap:] = chosen(slot[3 * cap :], grad[...])


def pick_rest(cap, slot, next_slot, grad, hid, next_grad, next_hid, near_g, near_h, far_h, near_pack):
    for own, other, value, next_value, out in (
        (0, 1, grad, next_grad, near_g),
        (0, 1, hid, next_hid, near_h),
        (2, 3, hid, next_hid, far_h),
    ):
        out[:cap] = chosen(slot[own * cap : (own + 1) * cap], value[...])
        out[cap:] = chosen(next_slot[other * cap : (other + 1) * cap], next_value[...])
    cols, share = near_g.shape[1], near_h.shape[1] // 2
    near_pack[:, :cols] = near_g[...]
    near_pack[:, cols:] = near_h[:, other_share(share)]


def own_share(share):
    return pl.ds(pl.multiple_of(lax.axis_index("dp") * share, share), share)


def other_share(share):
    return pl.ds(pl.multiple_of((1 - lax.axis_index("dp")) * share, share), share)


def cut_other(hid, out):
    out[...] = hid[:, other_share(out.shape[1])]


def hidden_grad(weight, i, grads, out):
    rows = weight.shape[1]
    part = lax.dot_general(grads[...], weight[i], (((1,), (1,)), ((), ())), preferred_element_type=jnp.float32)
    out[:, i * rows : (i + 1) * rows] = part.astype(out.dtype)


def output_rows(first, weight, hids, total):
    blocks, rows, _ = weight.shape
    for i in range(blocks):
        block = jnp.bitwise_xor(lax.axis_index("tensor"), first + 2 * i)
        start = pl.multiple_of(block * rows, rows)
        term = jnp.dot(hids[:, pl.ds(start, rows)], weight[i], preferred_element_type=jnp.float32)
        total = term if total is None else total + term
    return total


def weight_copies(first, weight, held, sem):
    rows = held.shape[1]
    copies = []
    for i in range(held.shape[0]):
        block = jnp.bitwise_xor(lax.axis_index("tensor"), first + 2 * i)
        start = pl.multiple_of(block * rows, rows)
        copies.append(pltpu.make_async_copy(weight.at[0, pl.ds(start, rows)], held.at[i], sem.at[i]))
        copies[i].start()
    return copies


def near_odd(weight, grads, slot, odd, send, slot_of_token, sem):
    copies = weight_copies(1, weight, odd, sem)
    tok = slot.shape[1]
    same = lax.broadcasted_iota(jnp.int32, (tok, tok), 0) == lax.broadcasted_iota(jnp.int32, (tok, tok), 1)
    slot_of_token[...] = lax.dot_general(
        jnp.where(same, 1.0, 0.0).astype(jnp.bfloat16),
        slot[...],
        (((1,), (1,)), ((), ())),
        preferred_element_type=jnp.float32,
    ).astype(jnp.bfloat16)
    for i, copy in enumerate(copies):
        copy.wait()
        hidden_grad(odd, i, grads, send)


def near_even(weight, odd, grads, hids, even, keep, own, following, sem):
    copies = weight_copies(0, weight, even, sem)
    total = output_rows(1, odd, hids, None)
    for i, copy in enumerate(copies):
        copy.wait()
        hidden_grad(even, i, grads, keep)
    cut_rows(output_rows(0, even, hids, total), (own, following))


def cut_rows(total, outs):
    rows = min(outs[0].shape[0], total.shape[0])
    for i, out in enumerate(outs):
        out[:rows] = total[i * rows : (i + 1) * rows].astype(out.dtype)
        if out.shape[0] > rows:
            out[rows:] = jnp.zeros((out.shape[0] - rows, out.shape[1]), out.dtype)


def far_grads(weight, grads, out):
    for i in range(weight.shape[0]):
        hidden_grad(weight, i, grads, out)


def far_outs(odd, even, hids, *outs):
    cut_rows(output_rows(0, even, hids, output_rows(1, odd, hids, None)), outs)


def fold(keep, got, *outs):
    total = keep[...] + got[...].astype(jnp.float32)
    if outs[0].dtype == jnp.float32:
        cut = outs[0].shape[1]
        outs[0][...] = total[:, :cut]
        outs[1][...] = total[:, cut:].astype(outs[1].dtype)
    else:
        cut_rows(total, outs)


def place(cap, slot, *refs):
    *rows, out, token = refs
    rows = [ref[...] if ref.shape[0] == cap else ref[i % 2 * cap : (i % 2 + 1) * cap] for i, ref in enumerate(rows)]
    out[...] = jnp.dot(
        slot[...], jnp.concatenate(rows, axis=0), preferred_element_type=jnp.float32
    ).astype(out.dtype)
    token[...] = jnp.zeros_like(token)


def outer_near(grads, hids, both, far_grads, far_hids, out):
    cols, share = grads.shape[1], out.shape[0]
    part = own_share(share)
    g = jnp.concatenate([grads[...], both[:, :cols], far_grads[...]], axis=0)
    h = jnp.concatenate([hids[:, part], both[:, cols:], far_hids[:, part]], axis=0)
    out[...] = lax.dot_general(h, g, (((0,), (0,)), ((), ())), preferred_element_type=jnp.float32)


def outer_far(near, grads, hids, out, token, held, sem):
    pieces, rows, _ = held.shape
    copies = []
    for i in range(pieces):
        part = slice(i * rows, (i + 1) * rows)
        term = lax.dot_general(
            hids[:, part], grads[...], (((0,), (0,)), ((), ())), preferred_element_type=jnp.float32
        )
        held[i] = (near[part] + term).astype(held.dtype)
        copies.append(pltpu.make_async_copy(held.at[i], out.at[0, pl.ds(i * rows, rows)], sem.at[i]))
        copies[i].start()
    token[...] = jnp.zeros_like(token)
    for copy in copies:
        copy.wait()


def few(hidden, out_grad, w_down, routes, placement):
    experts = lax.axis_size("expert")
    tensors = lax.axis_size("tensor")
    tok, width = hidden.shape
    cols = out_grad.shape[1]
    cap = 2 * tok // experts
    slots = experts * cap
    share = width // 2
    column = width // tensors
    bf, f32 = jnp.bfloat16, jnp.float32
    rows = 2 * cap
    kept, cut, token = (rows, width // 2), (rows, column), ((8, 128), f32)
    pair = ((cap, column), bf)

    routes = routes.reshape(1, tok)
    next_routes, next_grad, next_hid = (swap(x, "expert", 1) for x in (routes, out_grad, hidden))
    slot, table, grad, hid, far_g = call(
        functools.partial(pick_own, cap),
        [((slots, tok), bf), ((8, 128), jnp.int32), ((tok, cols), bf), ((tok, width), bf), ((cap, cols), bf)],
        tuple(far(x) for x in (routes, placement, out_grad, hidden)),
        [ANY] * 4,
        [
            pltpu.VMEM((1, tok), jnp.int32),
            pltpu.SMEM((experts,), jnp.int32),
            pltpu.SemaphoreType.DMA((4,)),
        ],
    )
    next_slot, far_g = call(
        functools.partial(pick_next, cap),
        [((slots, tok), bf), ((rows, cols), bf)],
        (table, next_routes, next_grad, far_g),
    )
    near_g, near_h, far_h, near_pack = call(
        functools.partial(pick_rest, cap),
        [((rows, cols), bf), ((rows, width), bf), ((rows, width), bf), ((rows, cols + share), bf)],
        (slot, next_slot, grad, hid, next_grad, next_hid),
    )
    far_h = swap(far_h, "expert", 2)
    far_g = swap(far_g, "expert", 2)
    other_near = swap(near_pack, "dp", 1)
    part = ((tensors // 2, column, cols), bf)
    sems = [pltpu.SemaphoreType.DMA((tensors // 2,))]
    odd, near_send, placer = call(
        near_odd,
        [part, (kept, bf), ((tok, slots), bf)],
        (far(w_down), near_g, slot),
        [ANY, VMEM, VMEM],
        sems,
    )
    near_got = swap(near_send, "tensor", 1)
    even, near_keep, near_out, next_out = call(
        near_even,
        [part, (kept, f32), ((cap, cols), bf), ((cap, cols), bf)],
        (far(w_down), odd, near_g, near_h),
        [ANY, *[VMEM] * 3],
        sems,
    )
    next_out = swap(next_out, "expert", 1)
    (far_send,) = call(far_grads, [(kept, bf)], (odd, far_g), after=(near_keep,))
    far_got = swap(far_send, "tensor", 1)
    other_g = swap(far_g, "dp", 1)
    last = far_send
    if tensors > 2:
        near_keep, near_send = call(fold, [(cut, f32), (cut, bf)], (near_keep, near_got), after=(last,))
        near_got = swap(near_send, "tensor", 2)
        last = near_send
    (far_keep,) = call(far_grads, [(kept, f32)], (even, far_g), after=(last,))
    last = far_keep
    far_out = call(far_outs, [((cap, cols), bf)] * 2, (odd, even, far_h), after=(last, next_out))
    last = far_out[0]
    if tensors > 2:
        far_keep, far_send = call(fold, [(cut, f32), (cut, bf)], (far_keep, far_got), after=(last, other_near))
        far_got = swap(far_send, "tensor", 2)
        last = far_send
    (cut_h,) = call(cut_other, [((rows, share), bf)], (far_h,), after=(last,))
    other_h = swap(cut_h, "dp", 1)
    (near_total,) = call(outer_near, [((share, cols), f32)], (near_g, near_h, other_near, far_g, far_h), after=(cut_h,))
    (near_back,) = call(fold, [((rows + 16, column), bf)], (near_keep, near_got), after=(near_total,))
    next_back = swap(near_back, "expert", 1)
    back = [swap(far_out[k], "expert", 2 + k) for k in (0, 1)][::-1]
    far_back = call(fold, [pair, pair], (far_keep, far_got), after=(near_back, other_g))
    output, last = call(
        functools.partial(place, cap),
        [((tok, cols), bf), token],
        (placer, near_out, next_out, back[1], back[0]),
        after=(far_back[0],),
    )
    pieces = 8
    d_weight, last = call(
        outer_far,
        [((1, share, cols), bf), token],
        (near_total, other_g, other_h),
        None,
        [pltpu.VMEM((pieces, share // pieces, cols), bf), pltpu.SemaphoreType.DMA((pieces,))],
        after=(last,),
        out_specs=[ANY, VMEM],
    )
    d_hidden, _ = call(
        functools.partial(place, cap),
        [((tok, column), bf), token],
        (
            placer,
            near_back,
            next_back,
            swap(far_back[0], "expert", 2),
            swap(far_back[1], "expert", 3),
        ),
        after=(last,),
    )
    return output, d_hidden, d_weight


def many(hidden, out_grad, w_down, routes, placement):
    experts = lax.axis_size("expert")
    tok = hidden.shape[0]
    width = hidden.shape[1]
    cols = out_grad.shape[1]
    cap = 2 * tok // experts
    slots = experts * cap
    target, within = route(routes, placement, experts, cap)
    position = target * cap + within
    picker = (jnp.arange(slots, dtype=jnp.int32)[:, None] == position[None, :]).astype(jnp.bfloat16)
    send_hidden = jnp.dot(picker, hidden, preferred_element_type=jnp.float32).astype(jnp.bfloat16)
    send_grad = jnp.dot(picker, out_grad, preferred_element_type=jnp.float32).astype(jnp.bfloat16)

    def exchange(value):
        return lax.all_to_all(
            value.reshape(experts, cap, -1), "expert", split_axis=0, concat_axis=0, tiled=True
        ).reshape(slots, -1)

    slot_hidden, slot_grad = exchange(send_hidden), exchange(send_grad)
    weight = w_down[0]
    out_rows = jnp.dot(slot_hidden, weight, preferred_element_type=jnp.float32).astype(jnp.bfloat16)
    partial_value = lax.dot_general(
        slot_grad, weight, (((1,), (1,)), ((), ())), preferred_element_type=jnp.float32
    )
    hidden_grad = lax.psum_scatter(partial_value, "tensor", scatter_dimension=1, tiled=True).astype(
        jnp.bfloat16
    )

    def place(rows):
        return jnp.einsum("rt,rd->td", picker, rows, preferred_element_type=jnp.float32).astype(jnp.bfloat16)

    output, d_hidden = place(exchange(out_rows)), place(exchange(hidden_grad))
    share = width // lax.axis_size("dp")
    mine = lax.axis_index("dp") * share
    part_h = lax.dynamic_slice_in_dim(
        lax.all_gather(slot_hidden, "dp", axis=0, tiled=True), mine, share, 1
    ).reshape(-1, slots, share)
    part_g = lax.all_gather(slot_grad, "dp", axis=0, tiled=True).reshape(-1, slots, cols)
    terms = jnp.einsum("krf,krd->kfd", part_h, part_g, preferred_element_type=jnp.float32)
    rounded = lax.optimization_barrier(terms.astype(jnp.bfloat16))
    summed = jnp.sum(rounded.astype(jnp.float32), axis=0)
    return output, d_hidden, summed.astype(jnp.bfloat16)[None]


def solution(mesh):
    in_specs = (
        P(("dp", "expert"), None),
        P(("dp", "expert"), "tensor"),
        P("expert", None, "tensor"),
        P(("dp", "expert"), None),
        P(),
    )
    out_specs = (
        P(("dp", "expert"), "tensor"),
        P(("dp", "expert"), "tensor"),
        P("expert", "dp", "tensor"),
    )
    small = mesh.shape["dp"] == 2 and mesh.shape["expert"] == 4 and mesh.shape["tensor"] in (2, 4)
    shards = few if small else many
    return jax.shard_map(shards, mesh=mesh, in_specs=in_specs, out_specs=out_specs, check_vma=False)
```

```python
import functools

import jax
import jax.numpy as jnp
from jax import lax
from jax.experimental import pallas as pl
from jax.experimental.pallas import tpu as pltpu
from jax.sharding import PartitionSpec as P

VMEM = pl.BlockSpec(memory_space=pltpu.VMEM)
ANY = pl.BlockSpec(memory_space=pl.ANY)


def call(kernel, outs, ins, specs=None, scratch=(), after=(), out_specs=None):
    name = getattr(kernel, "func", kernel).__name__

    def late(*refs):
        kernel(*refs[: len(ins)], *refs[len(ins) + len(after) :])

    return pl.pallas_call(
        late,
        out_shape=tuple(jax.ShapeDtypeStruct(s, d) for s, d in outs),
        in_specs=[*(specs or [VMEM] * len(ins)), *[ANY] * len(after)],
        out_specs=tuple(out_specs or [VMEM] * len(outs)),
        scratch_shapes=list(scratch),
        name=name,
        cost_estimate=pl.CostEstimate(flops=1000, bytes_accessed=1000, transcendentals=0),
        compiler_params=pltpu.CompilerParams(vmem_limit_bytes=24 << 20),
    )(*ins, *after)


def far(value):
    return pltpu.with_memory_space_constraint(value, pltpu.HBM)


def swap(value, axis, offset):
    size = lax.axis_size(axis)
    return lax.ppermute(value, axis, [(i, i ^ offset) for i in range(size)])


def route(routes, placement, experts, cap):
    chosen = routes == jnp.arange(placement.shape[0], dtype=jnp.int32)[None, :]
    target = jnp.sum(jnp.where(chosen, placement[None, :], 0), axis=1)
    landing = target[:, None] == jnp.arange(experts, dtype=jnp.int32)[None, :]
    counted = jnp.cumsum(landing.astype(jnp.int32), axis=0) - 1
    within = jnp.sum(jnp.where(landing, counted, 0), axis=1)
    return target, within


def slot_of(routes, placement, owner, experts, cap):
    tok = routes.shape[1]
    target = jnp.zeros((1, tok), jnp.int32)
    for j in range(experts):
        target = jnp.where(routes == j, placement[j : j + 1, :tok], target)
    key = jnp.bitwise_xor(target, owner)
    landing = jnp.where(key == lax.broadcasted_iota(jnp.int32, (max(8, experts), tok), 0), 1.0, 0.0)
    earlier = lax.broadcasted_iota(jnp.int32, (tok, tok), 0) <= lax.broadcasted_iota(jnp.int32, (tok, tok), 1)
    counted = jnp.dot(
        landing.astype(jnp.bfloat16),
        jnp.where(earlier, 1.0, 0.0).astype(jnp.bfloat16),
        preferred_element_type=jnp.float32,
    )
    within = jnp.sum(landing * counted, axis=0, keepdims=True).astype(jnp.int32) - 1
    position = key * cap + within
    slots = lax.broadcasted_iota(jnp.int32, (experts * cap, tok), 0)
    return jnp.where(position == slots, 1.0, 0.0).astype(jnp.bfloat16)


def chosen(slot, value):
    return jnp.dot(slot, value, preferred_element_type=jnp.float32).astype(jnp.bfloat16)


def pick_own(cap, routes, placement, grad, hid, slot_out, table, grad_out, hid_out, far_g, *refs):
    routes_held, placement_held, sem = refs
    copies = [
        pltpu.make_async_copy(*pair, sem.at[i])
        for i, pair in enumerate(
            ((routes, routes_held), (placement, placement_held), (grad, grad_out), (hid, hid_out))
        )
    ]
    for copy in copies:
        copy.start()
    copies[0].wait()
    copies[1].wait()
    experts = placement.shape[0]
    for j in range(experts):
        table[j : j + 1] = jnp.full((1, table.shape[1]), placement_held[j], jnp.int32)
    slot = slot_of(routes_held[...], table, lax.axis_index("expert"), experts, cap)
    slot_out[...] = slot
    copies[2].wait()
    far_g[...] = chosen(slot[2 * cap : 3 * cap], grad_out[...])
    copies[3].wait()


def pick_next(cap, table, routes, grad, own_far_g, slot_out, far_g):
    experts = lax.axis_size("expert")
    slot = slot_of(routes[...], table, jnp.bitwise_xor(lax.axis_index("expert"), 1), experts, cap)
    slot_out[...] = slot
    far_g[:cap] = own_far_g[...]
    far_g[cap:] = chosen(slot[3 * cap :], grad[...])


def pick_rest(cap, slot, next_slot, grad, hid, next_grad, next_hid, near_g, near_h, far_h, near_pack):
    for own, other, value, next_value, out in (
        (0, 1, grad, next_grad, near_g),
        (0, 1, hid, next_hid, near_h),
        (2, 3, hid, next_hid, far_h),
    ):
        out[:cap] = chosen(slot[own * cap : (own + 1) * cap], value[...])
        out[cap:] = chosen(next_slot[other * cap : (other + 1) * cap], next_value[...])
    cols, share = near_g.shape[1], near_h.shape[1] // 2
    near_pack[:, :cols] = near_g[...]
    near_pack[:, cols:] = near_h[:, other_share(share)]


def own_share(share):
    return pl.ds(pl.multiple_of(lax.axis_index("dp") * share, share), share)


def other_share(share):
    return pl.ds(pl.multiple_of((1 - lax.axis_index("dp")) * share, share), share)


def cut_other(hid, out):
    out[...] = hid[:, other_share(out.shape[1])]


def hidden_grad(weight, i, grads, out):
    rows = weight.shape[1]
    part = lax.dot_general(grads[...], weight[i], (((1,), (1,)), ((), ())), preferred_element_type=jnp.float32)
    out[:, i * rows : (i + 1) * rows] = part.astype(out.dtype)


def output_rows(first, weight, hids, total):
    blocks, rows, _ = weight.shape
    for i in range(blocks):
        block = jnp.bitwise_xor(lax.axis_index("tensor"), first + 2 * i)
        start = pl.multiple_of(block * rows, rows)
        term = jnp.dot(hids[:, pl.ds(start, rows)], weight[i], preferred_element_type=jnp.float32)
        total = term if total is None else total + term
    return total


def weight_copies(first, weight, held, sem):
    rows = held.shape[1]
    copies = []
    for i in range(held.shape[0]):
        block = jnp.bitwise_xor(lax.axis_index("tensor"), first + 2 * i)
        start = pl.multiple_of(block * rows, rows)
        copies.append(pltpu.make_async_copy(weight.at[0, pl.ds(start, rows)], held.at[i], sem.at[i]))
        copies[i].start()
    return copies


def near_odd(weight, grads, slot, odd, send, slot_of_token, sem):
    copies = weight_copies(1, weight, odd, sem)
    tok = slot.shape[1]
    same = lax.broadcasted_iota(jnp.int32, (tok, tok), 0) == lax.broadcasted_iota(jnp.int32, (tok, tok), 1)
    slot_of_token[...] = lax.dot_general(
        jnp.where(same, 1.0, 0.0).astype(jnp.bfloat16),
        slot[...],
        (((1,), (1,)), ((), ())),
        preferred_element_type=jnp.float32,
    ).astype(jnp.bfloat16)
    for i, copy in enumerate(copies):
        copy.wait()
        hidden_grad(odd, i, grads, send)


def near_even(weight, odd, grads, hids, even, keep, own, following, sem):
    copies = weight_copies(0, weight, even, sem)
    total = output_rows(1, odd, hids, None)
    for i, copy in enumerate(copies):
        copy.wait()
        hidden_grad(even, i, grads, keep)
    cut_rows(output_rows(0, even, hids, total), (own, following))


def cut_rows(total, outs):
    rows = min(outs[0].shape[0], total.shape[0])
    for i, out in enumerate(outs):
        out[:rows] = total[i * rows : (i + 1) * rows].astype(out.dtype)
        if out.shape[0] > rows:
            out[rows:] = jnp.zeros((out.shape[0] - rows, out.shape[1]), out.dtype)


def far_grads(weight, grads, out):
    for i in range(weight.shape[0]):
        hidden_grad(weight, i, grads, out)


def far_outs(odd, even, hids, *outs):
    cut_rows(output_rows(0, even, hids, output_rows(1, odd, hids, None)), outs)


def fold(keep, got, *outs):
    total = keep[...] + got[...].astype(jnp.float32)
    if outs[0].dtype == jnp.float32:
        cut = outs[0].shape[1]
        outs[0][...] = total[:, :cut]
        outs[1][...] = total[:, cut:].astype(outs[1].dtype)
    else:
        cut_rows(total, outs)


def place(cap, slot, *refs):
    *rows, out, token, held, sem = refs
    rows = [ref[...] if ref.shape[0] == cap else ref[i % 2 * cap : (i % 2 + 1) * cap] for i, ref in enumerate(rows)]
    rows = jnp.concatenate(rows, axis=0)
    pieces, _, size = held.shape
    copies = []
    for i in range(pieces):
        part = slice(i * size, (i + 1) * size)
        held[i] = jnp.dot(slot[...], rows[:, part], preferred_element_type=jnp.float32).astype(held.dtype)
        copies.append(pltpu.make_async_copy(held.at[i], out.at[:, pl.ds(i * size, size)], sem.at[i]))
        copies[i].start()
    token[...] = jnp.zeros_like(token)
    for copy in copies:
        copy.wait()


def outer_near(grads, hids, both, far_grads, far_hids, out):
    cols, share = grads.shape[1], out.shape[0]
    part = own_share(share)
    g = jnp.concatenate([grads[...], both[:, :cols], far_grads[...]], axis=0)
    h = jnp.concatenate([hids[:, part], both[:, cols:], far_hids[:, part]], axis=0)
    out[...] = lax.dot_general(h, g, (((0,), (0,)), ((), ())), preferred_element_type=jnp.float32)


def outer_far(near, grads, hids, out, token, held, sem):
    pieces, rows, _ = held.shape
    copies = []
    for i in range(pieces):
        part = slice(i * rows, (i + 1) * rows)
        term = lax.dot_general(
            hids[:, part], grads[...], (((0,), (0,)), ((), ())), preferred_element_type=jnp.float32
        )
        held[i] = (near[part] + term).astype(held.dtype)
        copies.append(pltpu.make_async_copy(held.at[i], out.at[0, pl.ds(i * rows, rows)], sem.at[i]))
        copies[i].start()
    token[...] = jnp.zeros_like(token)
    for copy in copies:
        copy.wait()


def few(hidden, out_grad, w_down, routes, placement):
    experts = lax.axis_size("expert")
    tensors = lax.axis_size("tensor")
    tok, width = hidden.shape
    cols = out_grad.shape[1]
    cap = 2 * tok // experts
    slots = experts * cap
    share = width // 2
    column = width // tensors
    bf, f32 = jnp.bfloat16, jnp.float32
    rows = 2 * cap
    kept, cut, token = (rows, width // 2), (rows, column), ((8, 128), f32)
    pair = ((cap, column), bf)

    routes = routes.reshape(1, tok)
    next_routes, next_grad, next_hid = (swap(x, "expert", 1) for x in (routes, out_grad, hidden))
    slot, table, grad, hid, far_g = call(
        functools.partial(pick_own, cap),
        [((slots, tok), bf), ((8, 128), jnp.int32), ((tok, cols), bf), ((tok, width), bf), ((cap, cols), bf)],
        tuple(far(x) for x in (routes, placement, out_grad, hidden)),
        [ANY] * 4,
        [
            pltpu.VMEM((1, tok), jnp.int32),
            pltpu.SMEM((experts,), jnp.int32),
            pltpu.SemaphoreType.DMA((4,)),
        ],
    )
    next_slot, far_g = call(
        functools.partial(pick_next, cap),
        [((slots, tok), bf), ((rows, cols), bf)],
        (table, next_routes, next_grad, far_g),
    )
    near_g, near_h, far_h, near_pack = call(
        functools.partial(pick_rest, cap),
        [((rows, cols), bf), ((rows, width), bf), ((rows, width), bf), ((rows, cols + share), bf)],
        (slot, next_slot, grad, hid, next_grad, next_hid),
    )
    far_h = swap(far_h, "expert", 2)
    far_g = swap(far_g, "expert", 2)
    other_near = swap(near_pack, "dp", 1)
    part = ((tensors // 2, column, cols), bf)
    sems = [pltpu.SemaphoreType.DMA((tensors // 2,))]
    odd, near_send, placer = call(
        near_odd,
        [part, (kept, bf), ((tok, slots), bf)],
        (far(w_down), near_g, slot),
        [ANY, VMEM, VMEM],
        sems,
    )
    near_got = swap(near_send, "tensor", 1)
    even, near_keep, near_out, next_out = call(
        near_even,
        [part, (kept, f32), ((cap, cols), bf), ((cap, cols), bf)],
        (far(w_down), odd, near_g, near_h),
        [ANY, *[VMEM] * 3],
        sems,
    )
    next_out = swap(next_out, "expert", 1)
    (far_send,) = call(far_grads, [(kept, bf)], (odd, far_g), after=(near_keep,))
    far_got = swap(far_send, "tensor", 1)
    other_g = swap(far_g, "dp", 1)
    last = far_send
    if tensors > 2:
        near_keep, near_send = call(fold, [(cut, f32), (cut, bf)], (near_keep, near_got), after=(last,))
        near_got = swap(near_send, "tensor", 2)
        last = near_send
    (far_keep,) = call(far_grads, [(kept, f32)], (even, far_g), after=(last,))
    last = far_keep
    far_out = call(far_outs, [((cap, cols), bf)] * 2, (odd, even, far_h), after=(last, next_out))
    last = far_out[0]
    if tensors > 2:
        far_keep, far_send = call(fold, [(cut, f32), (cut, bf)], (far_keep, far_got), after=(last, other_near))
        far_got = swap(far_send, "tensor", 2)
        last = far_send
    (cut_h,) = call(cut_other, [((rows, share), bf)], (far_h,), after=(last,))
    other_h = swap(cut_h, "dp", 1)
    (near_total,) = call(outer_near, [((share, cols), f32)], (near_g, near_h, other_near, far_g, far_h), after=(cut_h,))
    (near_back,) = call(fold, [((rows + 16, column), bf)], (near_keep, near_got), after=(near_total,))
    next_back = swap(near_back, "expert", 1)
    back = [swap(far_out[k], "expert", 2 + k) for k in (0, 1)][::-1]
    far_back = call(fold, [pair, pair], (far_keep, far_got), after=(near_back, other_g))
    output, last = call(
        functools.partial(place, cap),
        [((tok, cols), bf), token],
        (placer, near_out, next_out, back[1], back[0]),
        None,
        [pltpu.VMEM((2, tok, cols // 2), bf), pltpu.SemaphoreType.DMA((2,))],
        after=(far_back[0],),
        out_specs=[ANY, VMEM],
    )
    pieces = 8
    d_weight, last = call(
        outer_far,
        [((1, share, cols), bf), token],
        (near_total, other_g, other_h),
        None,
        [pltpu.VMEM((pieces, share // pieces, cols), bf), pltpu.SemaphoreType.DMA((pieces,))],
        after=(last,),
        out_specs=[ANY, VMEM],
    )
    d_hidden, _ = call(
        functools.partial(place, cap),
        [((tok, column), bf), token],
        (
            placer,
            near_back,
            next_back,
            swap(far_back[0], "expert", 2),
            swap(far_back[1], "expert", 3),
        ),
        None,
        [pltpu.VMEM((2, tok, column // 2), bf), pltpu.SemaphoreType.DMA((2,))],
        after=(last,),
        out_specs=[ANY, VMEM],
    )
    return output, d_hidden, d_weight


def many(hidden, out_grad, w_down, routes, placement):
    experts = lax.axis_size("expert")
    tok = hidden.shape[0]
    width = hidden.shape[1]
    cols = out_grad.shape[1]
    cap = 2 * tok // experts
    slots = experts * cap
    target, within = route(routes, placement, experts, cap)
    position = target * cap + within
    picker = (jnp.arange(slots, dtype=jnp.int32)[:, None] == position[None, :]).astype(jnp.bfloat16)
    send_hidden = jnp.dot(picker, hidden, preferred_element_type=jnp.float32).astype(jnp.bfloat16)
    send_grad = jnp.dot(picker, out_grad, preferred_element_type=jnp.float32).astype(jnp.bfloat16)

    def exchange(value):
        return lax.all_to_all(
            value.reshape(experts, cap, -1), "expert", split_axis=0, concat_axis=0, tiled=True
        ).reshape(slots, -1)

    slot_hidden, slot_grad = exchange(send_hidden), exchange(send_grad)
    weight = w_down[0]
    out_rows = jnp.dot(slot_hidden, weight, preferred_element_type=jnp.float32).astype(jnp.bfloat16)
    partial_value = lax.dot_general(
        slot_grad, weight, (((1,), (1,)), ((), ())), preferred_element_type=jnp.float32
    )
    hidden_grad = lax.psum_scatter(partial_value, "tensor", scatter_dimension=1, tiled=True).astype(
        jnp.bfloat16
    )

    def place(rows):
        return jnp.einsum("rt,rd->td", picker, rows, preferred_element_type=jnp.float32).astype(jnp.bfloat16)

    output, d_hidden = place(exchange(out_rows)), place(exchange(hidden_grad))
    share = width // lax.axis_size("dp")
    mine = lax.axis_index("dp") * share
    part_h = lax.dynamic_slice_in_dim(
        lax.all_gather(slot_hidden, "dp", axis=0, tiled=True), mine, share, 1
    ).reshape(-1, slots, share)
    part_g = lax.all_gather(slot_grad, "dp", axis=0, tiled=True).reshape(-1, slots, cols)
    terms = jnp.einsum("krf,krd->kfd", part_h, part_g, preferred_element_type=jnp.float32)
    rounded = lax.optimization_barrier(terms.astype(jnp.bfloat16))
    summed = jnp.sum(rounded.astype(jnp.float32), axis=0)
    return output, d_hidden, summed.astype(jnp.bfloat16)[None]


def solution(mesh):
    in_specs = (
        P(("dp", "expert"), None),
        P(("dp", "expert"), "tensor"),
        P("expert", None, "tensor"),
        P(("dp", "expert"), None),
        P(),
    )
    out_specs = (
        P(("dp", "expert"), "tensor"),
        P(("dp", "expert"), "tensor"),
        P("expert", "dp", "tensor"),
    )
    small = mesh.shape["dp"] == 2 and mesh.shape["expert"] == 4 and mesh.shape["tensor"] in (2, 4)
    shards = few if small else many
    return jax.shard_map(shards, mesh=mesh, in_specs=in_specs, out_specs=out_specs, check_vma=False)
```
